128 devices in a mesh: tm: 32 (over z, x, core), head: 4 (over y).
Axes of the slice: x: 4, y: 4, z: 4, core: 2. Of those that a mesh axis runs over, the one named last changes fastest.
Arguments:
- query: bfloat16 [98304, 1536], P('tm', 'head'), may hold values from -60 to 60
- keys: bfloat16 [98304, 1536], P('tm', 'head'), may hold values from -4 to 4
- values: bfloat16 [98304, 1536], P('tm', 'head'), may hold values from -6 to 6
- out_weight: bfloat16 [1536, 1536], P('head'), may hold values from -0.5 to 0.5
- near_list: int32 [768, 16], P('tm'), may hold values from 0 to 767, as said below
- far_list: int32 [768, 16], replicated, may hold values from 0 to 767, as said below
- stride_table: int32 [64], replicated, may hold values from 1 to 64, as said below
Outputs:
- mixed: bfloat16 [98304, 1536], P(('tm', 'head'))
The draws below stay inside these ranges and needn't reach their ends.
Inputs may be any that keep to these rules, and one draw needn't show every extreme that they name: `near_list`: row b lists 16 different blocks, the first being b itself, all in the frame of block b or the frames just before and after it. `far_list`: row b lists 16 different blocks. Over all query blocks held by one index of tm together, the listed blocks are exactly 6 blocks of every tm index two or more away from it and none of any other index. `stride_table`: entry d is 1 for d < 2 and one of 16, 32, 64 otherwise; entry 2 is 16 and the last entry is 64.
All inputs are finite; a program needn't handle non-finite values.
Results may differ from the reference program's by a relative error of at most 0.013.
Values may be sent and summed in bfloat16 or wider, within the bound.
No kernel may reach another device: no remote copies, remote signals or barrier semaphores. Data moves between devices by JAX's collectives and lax.ppermute only.
A program may use at most 128 MiB of HBM per device.

```python
import math
import jax
import jax.numpy as jnp
from jax import lax

D = 1536
H = 12
HD = 128
BLK = 128
FRAME_BLK = 12
KNEAR = 16
KFAR = 16
CAP = 6
MINSTRIDE = 16
TOK_DEV = 3072
TOKENS = 98304
FRAMES = 64
N_HEAD = 4


def shared_noise(key):
    first_key = jax.random.fold_in(key, 0)
    shape = (TOKENS, H * HD)
    return jax.random.normal(first_key, shape, jnp.float32)


def draw_keys(key, part):
    normal_part = shared_noise(key)
    return jnp.clip(normal_part, -4.0, 4.0).astype(jnp.bfloat16)


def draw_query(key, part):
    key = jax.random.fold_in(key, 5)
    own_normal = shared_noise(key)
    return jnp.clip(2.0 * own_normal, -8.0, 8.0).astype(jnp.bfloat16)


def draw_near_list(key, part):
    key = jax.random.fold_in(key, 11)
    block_count = TOKENS // BLK
    span = 3 * FRAME_BLK
    blocks = jnp.arange(block_count, dtype=jnp.int32)
    frame = blocks // FRAME_BLK
    candidate = (frame[:, None] - 1) * FRAME_BLK + jnp.arange(span, dtype=jnp.int32)[None, :]
    allowed = (candidate >= 0) & (candidate < block_count) & (candidate != blocks[:, None])
    ranking = jax.random.randint(key, (block_count, span), 0, 65536, jnp.int32) * 64 + jnp.arange(span, dtype=jnp.int32)[None, :]
    ranking = jnp.where(allowed, ranking, -1)
    _, chosen_at = lax.top_k(ranking, KNEAR - 1)
    chosen = jnp.take_along_axis(candidate, chosen_at, axis=1)
    return jnp.concatenate([blocks[:, None], chosen], axis=1).astype(jnp.int32)


def draw_far_list(key, part):
    key = jax.random.fold_in(key, 23)
    first_key, second_key = jax.random.split(key)
    device_count = TOKENS // TOK_DEV
    blocks = TOK_DEV // BLK
    devices = jnp.arange(device_count, dtype=jnp.int32)
    visible_score = jax.random.randint(first_key, (device_count, device_count, blocks), 0, 65536, jnp.int32) * 256 + jnp.arange(blocks, dtype=jnp.int32)
    _, picked = lax.top_k(visible_score, CAP)
    global_ids = (devices[None, :, None] * blocks + picked).reshape(device_count, device_count * CAP)
    distant = jnp.abs(devices[:, None] - devices[None, :]) >= 2
    distant = jnp.broadcast_to(distant[:, :, None], (device_count, device_count, CAP)).reshape(device_count, device_count * CAP)
    order_key = jax.random.randint(second_key, (device_count, device_count * CAP), 0, 65536, jnp.int32) * 4096 + jnp.arange(device_count * CAP, dtype=jnp.int32)
    order_key = jnp.where(distant, order_key, 1 << 30)
    ordering = jnp.argsort(order_key, axis=1, stable=True)
    listing = jnp.take_along_axis(global_ids, ordering, axis=1)
    count = jnp.sum(distant.astype(jnp.int32), axis=1)
    position = jnp.arange(blocks * KFAR, dtype=jnp.int32)[None, :] % count[:, None]
    chosen = jnp.take_along_axis(listing, position, axis=1)
    return chosen.reshape(device_count * blocks, KFAR).astype(jnp.int32)


def draw_stride_table(key, part):
    key = jax.random.fold_in(key, 37)
    exponent = jax.random.randint(key, (FRAMES,), 0, 3, jnp.int32)
    distance = jnp.arange(FRAMES, dtype=jnp.int32)
    table = MINSTRIDE * jnp.where(exponent == 0, 1, jnp.where(exponent == 1, 2, 4))
    table = jnp.where(distance < 2, 1, table)
    table = jnp.where(distance == 2, MINSTRIDE, table)
    table = jnp.where(distance == FRAMES - 1, 4 * MINSTRIDE, table)
    return table.astype(jnp.int32)


def shard_levels(key, shape, shards, least, largest):
    factor_of = 1.0
    for dim, shards_of in shards:
        steps = jax.random.uniform(jax.random.fold_in(jax.random.fold_in(key, 6), dim), (shards_of,), jnp.float32, least / len(shards), largest / len(shards))
        factor_of = factor_of * jnp.repeat(jnp.exp(steps), shape[dim] // shards_of).reshape((-1,) + (1,) * (len(shape) - 1 - dim))
    return factor_of


def noise(stream_key, shape, width, bound, cuts=(), kind=jnp.bfloat16):
    level = shard_levels(stream_key, shape, cuts, -0.22, 0.18) if cuts else 1.0
    array = jax.random.normal(stream_key, shape, jnp.float32) * width * level
    return jnp.minimum(jnp.maximum(array, -bound), bound).astype(kind)


def setup_inputs(seed: int = 0) -> dict:
    key_of = jax.random.split(jax.random.key(seed), 8)
    return {
        "query": draw_query(jax.random.fold_in(key_of[7], 71), 0),
        "keys": draw_keys(jax.random.fold_in(key_of[7], 71), 0),
        "values": noise(key_of[2], (TOKENS, H * HD), 1.0, 6.0, ((0, 32), (1, 4))),
        "out_weight": noise(key_of[3], (H * HD, D), HD ** -0.5, 0.5, ((0, 4),)),
        "near_list": draw_near_list(jax.random.fold_in(key_of[7], 71), 0),
        "far_list": draw_far_list(jax.random.fold_in(key_of[7], 71), 0),
        "stride_table": draw_stride_table(jax.random.fold_in(key_of[7], 71), 0),
    }


def reference(query, keys, values, out_weight, near_list, far_list, stride_table):
    block_count = TOKENS // BLK
    thin_rows = BLK // MINSTRIDE
    query_blocks = query.reshape(block_count, BLK, H, HD)
    key_blocks = keys.reshape(block_count, BLK, H, HD)
    value_blocks = values.reshape(block_count, BLK, H, HD)
    key_thin = key_blocks[:, ::MINSTRIDE]
    value_thin = value_blocks[:, ::MINSTRIDE]
    offsets = jnp.arange(thin_rows, dtype=jnp.int32) * MINSTRIDE
    scale = 1.0 / math.sqrt(HD)

    def one_block(block):
        near = near_list[block]
        far = far_list[block]
        keys_near = key_blocks[near].reshape(KNEAR * BLK, H, HD)
        values_near = value_blocks[near].reshape(KNEAR * BLK, H, HD)
        keys_far = key_thin[far].reshape(KFAR * thin_rows, H, HD)
        values_far = value_thin[far].reshape(KFAR * thin_rows, H, HD)
        distance = jnp.abs(block // FRAME_BLK - far // FRAME_BLK)
        stride = stride_table[distance]
        used = (offsets[None, :] % stride[:, None] == 0).reshape(-1)
        usable = jnp.concatenate([jnp.ones((KNEAR * BLK,), jnp.bool_), used])
        key_rows = jnp.concatenate([keys_near, keys_far], axis=0).astype(jnp.float32)
        value_rows = jnp.concatenate([values_near, values_far], axis=0).astype(jnp.float32)
        scores = jnp.einsum('qhd,khd->hqk', query_blocks[block].astype(jnp.float32), key_rows) * scale
        scores = jnp.where(usable[None, None, :], scores, -1e+30)
        row_peak = lax.optimization_barrier(jnp.max(scores, axis=-1, keepdims=True))
        weights = jnp.exp(scores - row_peak)
        totals = lax.optimization_barrier(jnp.sum(weights, axis=-1))
        rounded = lax.optimization_barrier(weights.astype(jnp.bfloat16)).astype(jnp.float32)
        attended = jnp.einsum('hqk,khd->qhd', rounded, value_rows) / jnp.transpose(totals)[..., None]
        return attended.astype(jnp.bfloat16).reshape(BLK, H * HD)
    attended = lax.map(one_block, jnp.arange(block_count, dtype=jnp.int32)).reshape(TOKENS, H * HD)
    group_width = H * HD // N_HEAD
    summed = jnp.zeros((TOKENS, D), jnp.float32)
    for group in range(N_HEAD):
        lower = group * group_width
        partial_term = jnp.dot(attended[:, lower:lower + group_width], out_weight[lower:lower + group_width], preferred_element_type=jnp.float32)
        summed = summed + lax.optimization_barrier(partial_term.astype(jnp.bfloat16)).astype(jnp.float32)
    return summed.astype(jnp.bfloat16)
```

```python
import functools
import math

import jax
import jax.numpy as jnp
from jax import lax
from jax.experimental import pallas as pl
from jax.experimental.pallas import tpu as pltpu
from jax.sharding import PartitionSpec as P

HD = 128
BLK = 128
FRAME_BLK = 12
KNEAR = 16
KFAR = 16
CAP = 6
MINSTRIDE = 16
THIN = BLK // MINSTRIDE
HEADS = 3
WIDTH = HEADS * HD
BLOCKS = 24
NX, NZ, NC = 4, 4, 2
NTM = NX * NZ * NC
NHEAD = 4
CHUNK = BLOCKS // NHEAD
FRAME = FRAME_BLK * BLK
LOG2_SCALE = math.log2(math.e) / math.sqrt(HD)
NT = (((1,), (1,)), ((), ()))
VMEM_LIMIT = 56 * 2**20


def tm_index(z, x, c):
    return (z % NZ) * NX * NC + (x % NX) * NC + c


def far_block(far_vm, slots, strides, base):
    tiles = [
        far_vm[pl.ds(pl.multiple_of(slots[base + j] * 2 * THIN, 2 * THIN), 2 * THIN), :].astype(
            jnp.float32
        )
        for j in range(KFAR)
    ]
    keys = jnp.concatenate([t[:THIN] for t in tiles], axis=0).astype(jnp.bfloat16)
    values = jnp.concatenate([t[THIN:] for t in tiles], axis=0).astype(jnp.bfloat16)
    lane = lax.broadcasted_iota(jnp.int32, (1, BLK), 1)
    stride = jnp.zeros((1, BLK), jnp.int32)
    for j in range(KFAR):
        stride = jnp.where(lane // THIN == j, strides[base + j], stride)
    used = (((lane % THIN) * MINSTRIDE) & (stride - 1)) == 0
    return keys, values, used


def with_ones(values):
    return jnp.concatenate([values, jnp.ones((values.shape[0], HD), jnp.bfloat16)], axis=1)


def attend_kernel(
    scalars, near, slots, strides, q_ref, k_ref, v_ref, halo_ref, *rest, per_step, with_far
):
    if with_far:
        far_refs, (out_ref, k_vm, v_vm, far_vm, sems) = rest[:8], rest[8:]
    else:
        acc_ref, stat_ref, k_vm, v_vm, sems = rest
    step = pl.program_id(0)
    own = BLOCKS * BLK

    @pl.when(step == 0)
    def _():
        copies = [
            pltpu.make_async_copy(k_ref, k_vm.at[pl.ds(0, own)], sems.at[0]),
            pltpu.make_async_copy(v_ref, v_vm.at[pl.ds(0, own)], sems.at[1]),
            pltpu.make_async_copy(halo_ref.at[0], k_vm.at[pl.ds(own, FRAME)], sems.at[2]),
            pltpu.make_async_copy(halo_ref.at[1], v_vm.at[pl.ds(own, FRAME)], sems.at[3]),
        ]
        if with_far:
            rows = far_refs[0].shape[0]
            for n, ref in enumerate(far_refs):
                copies.append(
                    pltpu.make_async_copy(ref, far_vm.at[pl.ds(n * rows, rows)], sems.at[4 + n])
                )
        for copy in copies:
            copy.start()
        for copy in copies:
            copy.wait()

    first = scalars[0] + step * per_step
    prepared = {}

    def prepare(unit):
        if unit not in prepared:
            base = (first + unit) * KNEAR
            offsets = [pl.multiple_of(near[base + j] * BLK, BLK) for j in range(KNEAR)]
            far = far_block(far_vm, slots, strides, base) if with_far else None
            prepared[unit] = offsets, far
        return prepared[unit]

    def scores_of(unit, head):
        offsets, far = prepare(unit)
        cols = slice(head * HD, head * HD + HD)
        query = q_ref[unit * BLK : unit * BLK + BLK, cols]
        scores = []
        for j in range(0, KNEAR, 2):
            keys = jnp.concatenate([k_vm[pl.ds(o, BLK), cols] for o in offsets[j : j + 2]], axis=0)
            both = lax.dot_general(query, keys, NT, preferred_element_type=jnp.float32)
            scores += [both[:, :BLK], both[:, BLK:]]
        if with_far:
            last = lax.dot_general(query, far[0][:, cols], NT, preferred_element_type=jnp.float32)
            scores.append(jnp.where(far[2], last, -1e30))
        return scores

    def finish(unit, head, scores):
        offsets, far = prepare(unit)
        cols = slice(head * HD, head * HD + HD)
        rows = slice(unit * BLK, unit * BLK + BLK)
        peak = (
            jnp.max(functools.reduce(jnp.maximum, scores), axis=1, keepdims=True) * LOG2_SCALE
        )
        acc = jnp.zeros((BLK, 2 * HD), jnp.float32)
        for j in range(0, len(scores), 2):
            some = range(j, min(j + 2, len(scores)))
            weights = jnp.concatenate(
                [jnp.exp2(scores[i] * LOG2_SCALE - peak).astype(jnp.bfloat16) for i in some], axis=1
            )
            values = jnp.concatenate(
                [
                    v_vm[pl.ds(offsets[i], BLK), cols] if i < KNEAR else far[1][:, cols]
                    for i in some
                ],
                axis=0,
            )
            acc += jnp.dot(weights, with_ones(values), preferred_element_type=jnp.float32)
        if with_far:
            out_ref[rows, cols] = (acc[:, :HD] / acc[:, HD : HD + 1]).astype(jnp.bfloat16)
        else:
            acc_ref[rows, cols] = acc[:, :HD]
            lane = lax.broadcasted_iota(jnp.int32, (BLK, HD), 1)
            held = stat_ref[rows, :] if head else jnp.zeros((BLK, HD), jnp.float32)
            held = jnp.where(lane == head, peak, held)
            stat_ref[rows, :] = jnp.where(lane == HEADS + head, acc[:, HD:], held)

    pending = None
    for unit in range(per_step):
        for head in range(HEADS):
            scores = scores_of(unit, head)
            if pending:
                finish(*pending)
            pending = unit, head, scores
    finish(*pending)


def attend(scalars, near, slots, strides, query, keys, values, halo, far, blocks, per_step):
    with_far = far is not None
    spot = lambda i, s, *_: (s[0] // per_step + i, 0)
    same = lambda i, *_: (i, 0)
    anywhere = pl.BlockSpec(memory_space=pl.ANY)
    rows = blocks * BLK
    step_rows = per_step * BLK
    scratch = [pltpu.VMEM((BLOCKS * BLK + FRAME, WIDTH), jnp.bfloat16) for _ in range(2)]
    if with_far:
        scratch.append(pltpu.VMEM((8 * far[0].shape[0], WIDTH), jnp.bfloat16))
        out_shape = jax.ShapeDtypeStruct((rows, WIDTH), jnp.bfloat16)
        out_specs = pl.BlockSpec((step_rows, WIDTH), same)
    else:
        out_shape = (
            jax.ShapeDtypeStruct((rows, WIDTH), jnp.float32),
            jax.ShapeDtypeStruct((rows, HD), jnp.float32),
        )
        out_specs = (pl.BlockSpec((step_rows, WIDTH), same), pl.BlockSpec((step_rows, HD), same))
    scratch.append(pltpu.SemaphoreType.DMA((12,)))
    extra = tuple(far) if with_far else ()
    return pl.pallas_call(
        functools.partial(attend_kernel, per_step=per_step, with_far=with_far),
        grid_spec=pltpu.PrefetchScalarGridSpec(
            num_scalar_prefetch=4,
            grid=(blocks // per_step,),
            in_specs=[pl.BlockSpec((step_rows, WIDTH), spot)] + [anywhere] * (3 + len(extra)),
            out_specs=out_specs,
            scratch_shapes=scratch,
        ),
        out_shape=out_shape,
        compiler_params=pltpu.CompilerParams(vmem_limit_bytes=VMEM_LIMIT),
        cost_estimate=pl.CostEstimate(
            flops=blocks * HEADS * 17 * 4 * BLK * BLK * HD * 3,
            bytes_accessed=8 * 2**20,
            transcendentals=0,
        ),
    )(scalars, near, slots, strides, query, keys, values, halo, *extra)


def merge_kernel(scalars, slots, strides, q_ref, acc_ref, stat_ref, *rest, per_step):
    far_refs, (out_ref, far_vm, sems) = rest[:8], rest[8:]
    step = pl.program_id(0)

    @pl.when(step == 0)
    def _():
        rows = far_refs[0].shape[0]
        copies = [
            pltpu.make_async_copy(ref, far_vm.at[pl.ds(n * rows, rows)], sems.at[n])
            for n, ref in enumerate(far_refs)
        ]
        for copy in copies:
            copy.start()
        for copy in copies:
            copy.wait()

    first = scalars[0] + step * per_step
    for unit in range(per_step):
        keys, values, used = far_block(far_vm, slots, strides, (first + unit) * KFAR)
        rows = slice(unit * BLK, unit * BLK + BLK)
        for head in range(HEADS):
            cols = slice(head * HD, head * HD + HD)
            scores = lax.dot_general(
                q_ref[rows, cols], keys[:, cols], NT, preferred_element_type=jnp.float32
            )
            scores = jnp.where(used, scores, -1e30) * LOG2_SCALE
            held = stat_ref[rows, head : head + 1]
            peak = jnp.maximum(jnp.max(scores, axis=1, keepdims=True), held)
            weights = jnp.exp2(scores - peak).astype(jnp.bfloat16)
            acc = jnp.dot(weights, with_ones(values[:, cols]), preferred_element_type=jnp.float32)
            shrink = jnp.exp2(held - peak)
            total = shrink * stat_ref[rows, HEADS + head : HEADS + head + 1] + acc[:, HD : HD + 1]
            mixed = shrink * acc_ref[rows, cols] + acc[:, :HD]
            out_ref[rows, cols] = (mixed / total).astype(jnp.bfloat16)


def merge_far(scalars, slots, strides, query, acc, stat, far, blocks, per_step):
    spot = lambda i, s, *_: (s[0] // per_step + i, 0)
    same = lambda i, *_: (i, 0)
    step_rows = per_step * BLK
    return pl.pallas_call(
        functools.partial(merge_kernel, per_step=per_step),
        grid_spec=pltpu.PrefetchScalarGridSpec(
            num_scalar_prefetch=3,
            grid=(blocks // per_step,),
            in_specs=[
                pl.BlockSpec((step_rows, WIDTH), spot),
                pl.BlockSpec((step_rows, WIDTH), same),
                pl.BlockSpec((step_rows, HD), same),
            ]
            + [pl.BlockSpec(memory_space=pl.ANY)] * 8,
            out_specs=pl.BlockSpec((step_rows, WIDTH), same),
            scratch_shapes=[
                pltpu.VMEM((8 * far[0].shape[0], WIDTH), jnp.bfloat16),
                pltpu.SemaphoreType.DMA((8,)),
            ],
        ),
        out_shape=jax.ShapeDtypeStruct((blocks * BLK, WIDTH), jnp.bfloat16),
        compiler_params=pltpu.CompilerParams(vmem_limit_bytes=VMEM_LIMIT),
        cost_estimate=pl.CostEstimate(
            flops=blocks * HEADS * 4 * BLK * BLK * HD * 6, bytes_accessed=8 * 2**20, transcendentals=0
        ),
    )(scalars, slots, strides, query, acc, stat, *far)


def select_kernel(picks, *refs):
    sources, outs = refs[:NX], refs[NX:]
    per = NX * CAP
    for n, out in enumerate(outs):

        def move(i, _, n=n, out=out):
            for s in range(NX):
                block = picks[n * per + s * CAP + i]
                at = pl.ds(pl.multiple_of(block * 2 * THIN, 2 * THIN), 2 * THIN)
                to = pl.ds(pl.multiple_of((s * CAP + i) * 2 * THIN, 2 * THIN), 2 * THIN)
                out[to, :] = sources[s][at, :]
            return 0

        lax.fori_loop(0, CAP, move, 0, unroll=True)


def select(picks, sources):
    shape = jax.ShapeDtypeStruct((NX * CAP * 2 * THIN, WIDTH), jnp.bfloat16)
    whole = lambda a: pl.BlockSpec(a.shape, lambda i, *_: (0, 0))
    return pl.pallas_call(
        select_kernel,
        grid_spec=pltpu.PrefetchScalarGridSpec(
            num_scalar_prefetch=1,
            grid=(1,),
            in_specs=[whole(s) for s in sources],
            out_specs=[whole(shape)] * (NZ * NC),
        ),
        out_shape=[shape] * (NZ * NC),
        compiler_params=pltpu.CompilerParams(vmem_limit_bytes=VMEM_LIMIT),
    )(picks, *sources)


def project_kernel(scalars, a0, a1, a2, a3, w0, w1, w2, w3, out_ref):
    total = None
    for a, w in ((a0, w0), (a1, w1), (a2, w2), (a3, w3)):
        part = jnp.dot(a[...], w[0, 0], preferred_element_type=jnp.float32)
        part = part.astype(jnp.bfloat16).astype(jnp.float32)
        total = part if total is None else total + part
    out_ref[...] = total.astype(jnp.bfloat16)


def project(scalars, parts, weights):
    halves, _, depth, cols = weights.shape
    rows = parts[0].shape[0]
    tile = rows // 3
    weight_spec = lambda n: pl.BlockSpec((1, 1, depth, cols), lambda c, r, s: (c, s[n], 0, 0))
    return pl.pallas_call(
        project_kernel,
        grid_spec=pltpu.PrefetchScalarGridSpec(
            num_scalar_prefetch=1,
            grid=(halves, 3),
            in_specs=[pl.BlockSpec((tile, depth), lambda c, r, s: (r, 0))] * NHEAD
            + [weight_spec(n) for n in range(NHEAD)],
            out_specs=pl.BlockSpec((tile, cols), lambda c, r, s: (r, c)),
        ),
        out_shape=jax.ShapeDtypeStruct((rows, halves * cols), jnp.bfloat16),
        compiler_params=pltpu.CompilerParams(vmem_limit_bytes=VMEM_LIMIT),
        cost_estimate=pl.CostEstimate(
            flops=2 * rows * NHEAD * depth * halves * cols,
            bytes_accessed=10 * 2**20,
            transcendentals=0,
        ),
    )(scalars, *parts, *([weights] * NHEAD))


def per_device(query, keys, values, out_weight, near_list, far_list, stride_table):
    t = lax.axis_index("tm")
    h = lax.axis_index("head")
    core, x, z = t % NC, (t // NC) % NX, t // (NC * NX)
    fast_frame = 1 - core
    coords = [(zz, xx, cc) for zz in range(NZ) for xx in range(NX) for cc in range(NC)]

    def thin(a):
        return a.reshape(BLOCKS, THIN, MINSTRIDE, WIDTH)[:, :, 0]

    thinned = jnp.concatenate([thin(keys), thin(values)], axis=1).reshape(-1, WIDTH)

    def frame_of(index):
        return jnp.stack(
            [lax.dynamic_slice_in_dim(a, index * FRAME, FRAME, 0) for a in (keys, values)]
        )

    swap = [(i, i ^ 1) for i in range(NTM)]
    across = [(i, i + 1) for i in range(1, NTM - 1, 2)]
    across = across + [(j, i) for i, j in across]
    along_x = [
        lax.ppermute(
            thinned, "tm", [(tm_index(*p), tm_index(p[0], p[1] + d, p[2])) for p in coords]
        )
        for d in range(1, NX)
    ]
    halo_fast = lax.ppermute(frame_of(fast_frame), "tm", swap)

    cols = out_weight.shape[1] // NC
    half = lax.dynamic_slice_in_dim(out_weight, core * cols, cols, 1)
    gathered = lax.all_gather(half, "head", axis=0)
    weights = lax.all_gather(
        gathered, "tm", axis=0, axis_index_groups=[[i, i + 1] for i in range(0, NTM, 2)]
    )

    listed = far_list.reshape(NTM, BLOCKS * KFAR)
    block_ids = jnp.arange(BLOCKS, dtype=jnp.int32)

    wanted = lax.dynamic_slice_in_dim(
        listed.reshape(NZ, NX, NC, -1), x, 1, 1
    )[:, 0]
    order = [(dz, dc) for dz in range(NZ) for dc in range(NC)]
    receivers = jnp.stack([((z + dz) % NZ) * NC + (core ^ dc) for dz, dc in order])
    wanted = wanted.reshape(NZ * NC, -1)[receivers]
    source = jnp.stack([tm_index(z, x - dx + NX, core) for dx in range(NX)])
    target = source[:, None] * BLOCKS + block_ids[None, :]
    present = jnp.any(wanted[:, None, None, :] == target[None, :, :, None], axis=-1)
    rank = jnp.cumsum(present.astype(jnp.int32), axis=-1) - 1
    hit = present[..., None] & (rank[..., None] == jnp.arange(CAP, dtype=jnp.int32))
    picks = jnp.sum(jnp.where(hit, block_ids[:, None], 0), axis=2).reshape(-1)

    mine = lax.dynamic_slice_in_dim(listed, t, 1, 0)[0]
    ids = jnp.arange(NTM * BLOCKS, dtype=jnp.int32)
    have = jnp.any(mine[:, None] == ids[None, :], axis=0).reshape(NTM, BLOCKS)
    place = jnp.cumsum(have.astype(jnp.int32), axis=-1) - 1
    device = jnp.arange(NTM, dtype=jnp.int32)
    dz = (z - device // (NX * NC)) % NZ
    dx = (x - (device // NC) % NX) % NX
    dc = core ^ (device % NC)
    lies = (((dz * NC + dc) * NX + dx) * CAP)[:, None] + place
    slots = jnp.sum(jnp.where(mine[:, None] == ids[None, :], lies.reshape(-1)[None, :], 0), axis=1)
    row_frame = (t * BLOCKS + jnp.arange(BLOCKS * KFAR, dtype=jnp.int32) // KFAR) // FRAME_BLK
    distance = jnp.abs(row_frame - mine // FRAME_BLK)
    frames = jnp.arange(stride_table.shape[0], dtype=jnp.int32)
    strides = jnp.sum(
        jnp.where(distance[:, None] == frames[None, :], stride_table[None, :], 0), axis=1
    )

    local = near_list - t * BLOCKS
    near = jnp.where(local < 0, local + FRAME_BLK + BLOCKS, local).reshape(-1)

    packs = select(picks, [thinned] + along_x)
    slow_part, packs = lax.optimization_barrier((frame_of(core), packs))
    far = [packs[0]]
    for n, (dz_, dc_) in enumerate(order):
        if n:
            pairs = [(tm_index(*p), tm_index(p[0] + dz_, p[1], p[2] ^ dc_)) for p in coords]
            far.append(lax.ppermute(packs[n], "tm", pairs))
    halo_slow = lax.ppermute(slow_part, "tm", across)

    def start_at(block):
        return jnp.stack([block]).astype(jnp.int32)

    fast_start = start_at(fast_frame * FRAME_BLK)
    acc, stat = attend(
        fast_start, near, slots, strides, query, keys, values, halo_fast, None, FRAME_BLK, 4
    )
    done_fast = merge_far(fast_start, slots, strides, query, acc, stat, far, FRAME_BLK, 4)

    slow_frame = core
    in_half = (h // 2) == slow_frame
    first_dest = jnp.where(in_half, h ^ 1, h ^ 2)
    last_dest = jnp.where(in_half, h, h ^ 3)
    early, late = [
        attend(
            start_at(dest * CHUNK),
            near,
            slots,
            strides,
            query,
            keys,
            values,
            halo_slow,
            far,
            CHUNK,
            CHUNK,
        )
        for dest in (first_dest, last_dest)
    ]

    def exchange(chunk, e, fast):
        pairs = []
        for c in range(NC):
            frame = 1 - c if fast else c
            for i in range(NTM):
                if i % NC == c:
                    for g in range(NHEAD):
                        if (e >= 2) == (g // 2 != frame):
                            pairs.append((i * NHEAD + g, i * NHEAD + (g ^ e)))
        return lax.ppermute(chunk, ("tm", "head"), pairs)

    def fast_chunk(dest):
        return lax.dynamic_slice_in_dim(done_fast, (dest % 2) * CHUNK * BLK, CHUNK * BLK, 0)

    gets_fast = (h // 2) == fast_frame
    parts = [jnp.where(gets_fast, fast_chunk(h), late)]
    for e, chunk in ((1, early), (2, early), (3, late)):
        received_fast = exchange(fast_chunk(h ^ e), e, True)
        received_slow = exchange(chunk, e, False)
        parts.append(jnp.where(gets_fast, received_fast, received_slow))
    scalars = jnp.stack([h, h ^ 1, h ^ 2, h ^ 3]).astype(jnp.int32)
    return project(scalars, parts, weights)


def solution(mesh):
    placed = (
        P("tm", "head"),
        P("tm", "head"),
        P("tm", "head"),
        P("head", None),
        P("tm", None),
        P(),
        P(),
    )
    return jax.shard_map(
        per_device, mesh=mesh, in_specs=placed, out_specs=P(("tm", "head"), None), check_vma=False
    )
```

```python
import functools
import math

import jax
import jax.numpy as jnp
from jax import lax
from jax.experimental import pallas as pl
from jax.experimental.pallas import tpu as pltpu
from jax.sharding import PartitionSpec as P

HD = 128
BLK = 128
FRAME_BLK = 12
KNEAR = 16
KFAR = 16
CAP = 6
MINSTRIDE = 16
THIN = BLK // MINSTRIDE
HEADS = 3
WIDTH = HEADS * HD
BLOCKS = 24
NX, NZ, NC = 4, 4, 2
NTM = NX * NZ * NC
NHEAD = 4
CHUNK = BLOCKS // NHEAD
FAR_ROWS = NTM * CAP * 2 * THIN
FRAME = FRAME_BLK * BLK
LOG2_SCALE = math.log2(math.e) / math.sqrt(HD)
NT = (((1,), (1,)), ((), ()))
VMEM_LIMIT = 56 * 2**20
UNROLL = 3
SLOT, STRIDE, ORDER = KNEAR, KNEAR + KFAR, BLOCKS
FAST_FIRST, FAST_LAST, SLOW_FIRST, SLOW_LAST = range(4)
IN_HBM = pl.BlockSpec(memory_space=pltpu.HBM)


def tm_index(z, x, c):
    return (z % NZ) * NX * NC + (x % NX) * NC + c


def load_far(far_refs, far_vm, sems, first_sem):
    part = NX * CAP * 2 * THIN
    copies = []
    for n, ref in enumerate(far_refs):
        rows = part if n < NZ else NZ * part
        copies.append(
            pltpu.make_async_copy(
                ref.at[pl.ds(0, rows)], far_vm.at[pl.ds(n * part, rows)], sems.at[first_sem + n]
            )
        )
    return copies


def far_block(far_vm, table, block):
    tiles = [
        far_vm[
            pl.ds(pl.multiple_of(table[block, SLOT + j] * 2 * THIN, 2 * THIN), 2 * THIN), :
        ].astype(jnp.float32)
        for j in range(KFAR)
    ]
    keys = jnp.concatenate([t[:THIN] for t in tiles], axis=0).astype(jnp.bfloat16)
    values = jnp.concatenate([t[THIN:] for t in tiles], axis=0).astype(jnp.bfloat16)
    lane = lax.broadcasted_iota(jnp.int32, (1, BLK), 1)
    stride = jnp.zeros((1, BLK), jnp.int32)
    for j in range(KFAR):
        stride = jnp.where(lane // THIN == j, table[block, STRIDE + j], stride)
    used = (((lane % THIN) * MINSTRIDE) & (stride - 1)) == 0
    return keys, values, used


def with_ones(values):
    return jnp.concatenate([values, jnp.ones((values.shape[0], HD), jnp.bfloat16)], axis=1)


def attend_kernel(table, q_ref, k_ref, v_ref, halo_ref, *rest, chunk, with_far):
    if with_far:
        far_refs, (out_ref, k_vm, v_vm, s_vm, far_vm, sems) = rest[:5], rest[5:]
    else:
        near_ref, level_ref, k_vm, v_vm, s_vm, sems = rest
    step = pl.program_id(0)
    own = BLOCKS * BLK
    halo = pl.ds(own, FRAME)
    key_copies = [
        pltpu.make_async_copy(k_ref, k_vm.at[pl.ds(0, own)], sems.at[0]),
        pltpu.make_async_copy(halo_ref.at[pl.ds(0, FRAME)], k_vm.at[halo], sems.at[1]),
    ]
    value_copies = [
        pltpu.make_async_copy(v_ref, v_vm.at[pl.ds(0, own)], sems.at[2]),
        pltpu.make_async_copy(halo_ref.at[pl.ds(FRAME, FRAME)], v_vm.at[halo], sems.at[3]),
    ]
    if with_far:
        key_copies += load_far(far_refs, far_vm, sems, 4)

    @pl.when(step == 0)
    def _():
        for copy in key_copies + value_copies:
            copy.start()
        for copy in key_copies:
            copy.wait()

    first = table[ORDER, chunk + step] * CHUNK

    def prepare(unit):
        block = first + unit
        offsets = [pl.multiple_of(table[block, j] * BLK, BLK) for j in range(KNEAR)]
        far = far_block(far_vm, table, block) if with_far else None
        return offsets, far, pl.ds(pl.multiple_of(unit * BLK, BLK), BLK)

    count = KNEAR + (1 if with_far else 0)

    def score_pair(prepared, head, j):
        offsets, far, rows = prepared
        cols = slice(head * HD, head * HD + HD)
        query = q_ref[rows, cols]
        if j < KNEAR:
            keys = jnp.concatenate([k_vm[pl.ds(o, BLK), cols] for o in offsets[j : j + 2]], axis=0)
            both = lax.dot_general(query, keys, NT, preferred_element_type=jnp.float32)
            return [both[:, :BLK], both[:, BLK:]]
        last = lax.dot_general(query, far[0][:, cols], NT, preferred_element_type=jnp.float32)
        return [jnp.where(far[2], last, -1e30)]

    def peak_of(scores):
        top = functools.reduce(jnp.maximum, scores)
        return jnp.max(top, axis=1, keepdims=True) * LOG2_SCALE

    def add_pair(acc, prepared, head, scores, peak, j):
        offsets, far, _ = prepared
        cols = slice(head * HD, head * HD + HD)
        some = range(j, min(j + 2, count))
        weights = jnp.concatenate(
            [jnp.exp2(scores[i] * LOG2_SCALE - peak).astype(jnp.bfloat16) for i in some], axis=1
        )
        values = jnp.concatenate(
            [v_vm[pl.ds(offsets[i], BLK), cols] if i < KNEAR else far[1][:, cols] for i in some],
            axis=0,
        )
        part = jnp.dot(weights, with_ones(values), preferred_element_type=jnp.float32)
        return part if acc is None else acc + part

    def store(prepared, head, peak, acc):
        rows = prepared[2]
        cols = slice(head * HD, head * HD + HD)
        if with_far:
            out_ref[rows, cols] = (acc[:, :HD] / acc[:, HD:]).astype(jnp.bfloat16)
        else:
            near_ref[rows, cols] = (acc[:, :HD] / acc[:, HD:]).astype(jnp.bfloat16)
            level_ref[rows, cols] = peak + jnp.log2(acc[:, HD:])

    def scores_of(prepared, head):
        scores = []
        for j in range(0, count, 2):
            scores += score_pair(prepared, head, j)
        return scores

    def overlap(fresh, pending):
        prepared, head, scores = pending
        peak = peak_of(scores)
        following, acc = [], None
        for j in range(0, count, 2):
            following += score_pair(*fresh, j)
            acc = add_pair(acc, prepared, head, scores, peak, j)
        store(prepared, head, peak, acc)
        return following

    def hold(scores):
        for i, some in enumerate(scores):
            s_vm[:, i * BLK : i * BLK + BLK] = some

    hold(scores_of(prepare(0), 0))

    @pl.when(step == 0)
    def _():
        for copy in value_copies:
            copy.wait()

    units = CHUNK // UNROLL

    def body(i, _):
        pending = None
        scores = [s_vm[:, n * BLK : n * BLK + BLK] for n in range(count)]
        for u in range(UNROLL):
            unit = i * UNROLL + u
            prepared = prepare(unit)
            for head in range(HEADS):
                if head or u:
                    scores = overlap((prepared, head), pending)
                pending = prepared, head, scores
        after = prepare(jnp.minimum(i * UNROLL + UNROLL, CHUNK - 1))
        hold(overlap((after, 0), pending))
        return 0

    lax.fori_loop(0, units, body, 0)


def attend(table, query, keys, values, halo, far, chunk, chunks):
    with_far = far is not None
    spot = lambda i, s: (s[ORDER, chunk + i], 0)
    same = lambda i, s: (i, 0)
    rows = CHUNK * BLK
    scratch = [pltpu.VMEM((BLOCKS * BLK + FRAME, WIDTH), jnp.bfloat16) for _ in range(2)]
    scratch.append(pltpu.VMEM((BLK, (KNEAR + 1) * BLK), jnp.float32))
    if with_far:
        scratch.append(pltpu.VMEM((FAR_ROWS, WIDTH), jnp.bfloat16))
        out_shape = jax.ShapeDtypeStruct((chunks * rows, WIDTH), jnp.bfloat16)
        out_specs = pl.BlockSpec((rows, WIDTH), same)
    else:
        out_shape = [
            jax.ShapeDtypeStruct((chunks * rows, WIDTH), kind)
            for kind in (jnp.bfloat16, jnp.float32)
        ]
        out_specs = [pl.BlockSpec((rows, WIDTH), same)] * 2
    scratch.append(pltpu.SemaphoreType.DMA((9,)))
    extra = tuple(far) if with_far else ()
    return pl.pallas_call(
        functools.partial(attend_kernel, chunk=chunk, with_far=with_far),
        grid_spec=pltpu.PrefetchScalarGridSpec(
            num_scalar_prefetch=1,
            grid=(chunks,),
            in_specs=[pl.BlockSpec((rows, WIDTH), spot)] + [IN_HBM] * (3 + len(extra)),
            out_specs=out_specs,
            scratch_shapes=scratch,
        ),
        out_shape=out_shape,
        compiler_params=pltpu.CompilerParams(vmem_limit_bytes=VMEM_LIMIT),
        cost_estimate=pl.CostEstimate(
            flops=chunks * CHUNK * HEADS * 17 * 4 * BLK * BLK * HD * 3,
            bytes_accessed=8 * 2**20,
            transcendentals=0,
        ),
    )(table, query, keys, values, halo, *extra)


def merge_kernel(table, q_ref, near_ref, level_ref, *rest, chunk):
    far_refs, (_, first_ref, last_ref, out_vm, far_vm, sems) = rest[:5], rest[5:]
    step = pl.program_id(0)

    @pl.when(step == 0)
    def _():
        copies = load_far(far_refs, far_vm, sems, 0)
        for copy in copies:
            copy.start()
        for copy in copies:
            copy.wait()

    first = table[ORDER, chunk + step] * CHUNK
    spot = {
        (unit, head): (
            slice(unit * BLK, unit * BLK + BLK),
            slice(head * HD, head * HD + HD),
        )
        for unit in range(CHUNK)
        for head in range(HEADS)
    }
    far = [far_block(far_vm, table, first + unit) for unit in range(CHUNK)]
    scores, peaks, sums = {}, {}, {}
    for p, (rows, cols) in spot.items():
        keys, _, used = far[p[0]]
        some = lax.dot_general(
            q_ref[rows, cols], keys[:, cols], NT, preferred_element_type=jnp.float32
        )
        scores[p] = jnp.where(used, some, -1e30) * LOG2_SCALE
    for p, (rows, cols) in spot.items():
        peaks[p] = jnp.maximum(jnp.max(scores[p], axis=1, keepdims=True), level_ref[rows, cols])
    for p, (rows, cols) in spot.items():
        weights = jnp.exp2(scores[p] - peaks[p]).astype(jnp.bfloat16)
        values = far[p[0]][1][:, cols]
        sums[p] = jnp.dot(weights, with_ones(values), preferred_element_type=jnp.float32)
    for p, (rows, cols) in spot.items():
        share = jnp.exp2(level_ref[rows, cols] - peaks[p])
        total = share + sums[p][:, HD:]
        mixed = near_ref[rows, cols].astype(jnp.float32) * share + sums[p][:, :HD]
        out_vm[step, rows, cols] = (mixed / total).astype(jnp.bfloat16)

    outs = [
        pltpu.make_async_copy(out_vm.at[n], ref, sems.at[5 + n])
        for n, ref in enumerate((first_ref, last_ref))
    ]

    @pl.when(step == 0)
    def _():
        outs[0].start()

    @pl.when(step == 1)
    def _():
        outs[1].start()
        for copy in outs:
            copy.wait()


def merge_far(table, query, state, far, chunk, after):
    rows = CHUNK * BLK
    return pl.pallas_call(
        functools.partial(merge_kernel, chunk=chunk),
        grid_spec=pltpu.PrefetchScalarGridSpec(
            num_scalar_prefetch=1,
            grid=(2,),
            in_specs=[pl.BlockSpec((rows, WIDTH), lambda i, s: (s[ORDER, chunk + i], 0))]
            + [pl.BlockSpec((rows, WIDTH), lambda i, s: (i, 0))] * 2
            + [IN_HBM] * 6,
            out_specs=[IN_HBM] * 2,
            scratch_shapes=[
                pltpu.VMEM((2, rows, WIDTH), jnp.bfloat16),
                pltpu.VMEM((FAR_ROWS, WIDTH), jnp.bfloat16),
                pltpu.SemaphoreType.DMA((7,)),
            ],
        ),
        out_shape=[jax.ShapeDtypeStruct((rows, WIDTH), jnp.bfloat16)] * 2,
        compiler_params=pltpu.CompilerParams(vmem_limit_bytes=VMEM_LIMIT),
        cost_estimate=pl.CostEstimate(
            flops=2 * CHUNK * HEADS * 4 * BLK * BLK * HD * 6,
            bytes_accessed=8 * 2**20,
            transcendentals=0,
        ),
    )(table, query, *state, *far, after)


def index_kernel(scalars, steps, far_ref, near_ref, picks_ref, table_ref):
    t = scalars[0]
    core, x, z = t & 1, (t >> 1) & 3, t >> 3
    lane = lax.broadcasted_iota(jnp.int32, (1, BLK), 1)
    group = (lane * 2731) >> 16
    within = lane - group * BLOCKS
    valid = lane < NX * BLOCKS

    source = ((z * NX + ((x - group) & 3)) * NC + core) * BLOCKS + within
    source = jnp.where(valid, source, -1)
    present = []
    for dz in range(NZ):
        for dc in range(NC):
            receiver = (((z + dz) & 3) * NX + x) * NC + (core ^ dc)
            listed = far_ref[pl.ds(pl.multiple_of(receiver * BLOCKS, 8), BLOCKS), :]
            found = jnp.zeros((BLOCKS, BLK), jnp.float32)
            for j in range(KFAR):
                found = jnp.where(listed[:, j : j + 1] == source, 1.0, found)
            present.append(jnp.max(found, axis=0, keepdims=True))

    mine = far_ref[pl.ds(pl.multiple_of(t * BLOCKS, 8), BLOCKS), :]
    ids = [jnp.where(valid, row * NX * BLOCKS + lane, -1) for row in range(NTM // NX)]
    found = [jnp.zeros((BLOCKS, BLK), jnp.float32) for _ in ids]
    for j in range(KFAR):
        column = jnp.broadcast_to(mine[:, j : j + 1], (BLOCKS, BLK))
        found = [jnp.where(column == i, 1.0, f) for i, f in zip(ids, found)]
    present += [jnp.max(f, axis=0, keepdims=True) for f in found]
    present = jnp.concatenate(present, axis=0)

    a = lax.broadcasted_iota(jnp.int32, (BLK, BLK), 0)
    b = lax.broadcasted_iota(jnp.int32, (BLK, BLK), 1)
    group_a, group_b = (a * 2731) >> 16, (b * 2731) >> 16
    before = jnp.where((group_a == group_b) & (a < b), 1.0, 0.0).astype(jnp.bfloat16)
    rank = jnp.dot(present.astype(jnp.bfloat16), before, preferred_element_type=jnp.float32)

    receivers = NZ * NC
    chosen = [
        jnp.where((present[:receivers] > 0) & (rank[:receivers] == k), within.astype(jnp.float32), 0.0)
        for k in range(CAP)
    ]
    gather = jnp.where(group_a == b, 1.0, 0.0).astype(jnp.bfloat16)
    picks = jnp.dot(
        jnp.concatenate(chosen, axis=0).astype(jnp.bfloat16),
        gather,
        preferred_element_type=jnp.float32,
    )
    picks_ref[...] = picks.astype(jnp.int32)

    lies = []
    for row in range(NTM // NX):
        device = row * NX + group
        dz = (z - (device >> 3)) & 3
        dx = (x - (device >> 1)) & 3
        dc = core ^ (device & 1)
        start = ((dc * NZ + dz) * NX + dx) * CAP
        lies.append(start.astype(jnp.float32) + rank[receivers + row : receivers + row + 1])
    entry = lax.broadcasted_iota(jnp.int32, (BLOCKS, KFAR), 1)
    slots = jnp.zeros((BLOCKS, KFAR), jnp.float32)
    for j in range(KFAR):
        column = jnp.broadcast_to(mine[:, j : j + 1], (BLOCKS, BLK))
        at = jnp.zeros((BLOCKS, BLK), jnp.float32)
        for i, where in zip(ids, lies):
            at = jnp.where(column == i, where, at)
        slots = jnp.where(entry == j, jnp.sum(at, axis=1, keepdims=True), slots)

    row = lax.broadcasted_iota(jnp.int32, (BLOCKS, KFAR), 0)
    frame = t * (BLOCKS // FRAME_BLK) + jnp.where(row >= FRAME_BLK, 1, 0)
    distance = jnp.abs(frame - ((mine * 5462) >> 16))
    strides = jnp.zeros((BLOCKS, KFAR), jnp.int32)
    for d in range(steps.shape[0]):
        strides = jnp.where(distance == d, steps[d], strides)

    local = near_ref[...] - t * BLOCKS
    local = jnp.where(local < 0, local + FRAME_BLK + BLOCKS, local)
    rest = jnp.zeros((BLOCKS, BLK - KNEAR - 2 * KFAR), jnp.int32)
    table_ref[:BLOCKS, :] = jnp.concatenate(
        [local, slots.astype(jnp.int32), strides, rest], axis=1
    )

    h = scalars[1]
    order = jnp.zeros((8, BLK), jnp.int32)
    column = lax.broadcasted_iota(jnp.int32, (8, BLK), 1)
    for at, half in ((FAST_FIRST, 1 - core), (SLOW_FIRST, core)):
        inside = (h >> 1) == half
        order = jnp.where(column == at, jnp.where(inside, h ^ 1, h ^ 2), order)
        order = jnp.where(column == at + 1, jnp.where(inside, h, h ^ 3), order)
    table_ref[BLOCKS:, :] = order


def index_work(scalars, steps, far_list, near_list):
    whole = lambda shape: pl.BlockSpec(shape, lambda i, *_: (0, 0))
    shapes = [(NZ * NC * CAP, BLK), (BLOCKS + 8, BLK)]
    return pl.pallas_call(
        index_kernel,
        grid_spec=pltpu.PrefetchScalarGridSpec(
            num_scalar_prefetch=2,
            grid=(1,),
            in_specs=[whole(far_list.shape), whole(near_list.shape)],
            out_specs=[whole(shape) for shape in shapes],
        ),
        out_shape=[jax.ShapeDtypeStruct(shape, jnp.int32) for shape in shapes],
        cost_estimate=pl.CostEstimate(flops=2**20, bytes_accessed=2**22, transcendentals=0),
    )(scalars, steps, far_list, near_list)


def halo_kernel(scalars, k_fast, v_fast, k_slow, v_slow, after, fast_ref, slow_ref):
    fast_ref[0] = k_fast[...]
    fast_ref[1] = v_fast[...]
    slow_ref[0] = k_slow[...]
    slow_ref[1] = v_slow[...]


def pack_halos(scalars, keys, values, after):
    parts = 4
    rows = FRAME // parts
    fast = pl.BlockSpec((rows, WIDTH), lambda i, s: ((1 - (s[0] & 1)) * parts + i, 0))
    slow = pl.BlockSpec((rows, WIDTH), lambda i, s: ((s[0] & 1) * parts + i, 0))
    shape = jax.ShapeDtypeStruct((2, FRAME, WIDTH), jnp.bfloat16)
    outs = pl.pallas_call(
        halo_kernel,
        grid_spec=pltpu.PrefetchScalarGridSpec(
            num_scalar_prefetch=1,
            grid=(parts,),
            in_specs=[fast, fast, slow, slow, IN_HBM],
            out_specs=[pl.BlockSpec((2, rows, WIDTH), lambda i, s: (0, i, 0))] * 2,
        ),
        out_shape=[shape] * 2,
        cost_estimate=pl.CostEstimate(flops=0, bytes_accessed=10 * 2**20, transcendentals=0),
    )(scalars, keys, values, keys, values, after)
    return [out.reshape(2 * FRAME, WIDTH) for out in outs]


def pass_kernel(a, b, c, d, after, out_ref):
    rows = a.shape[0]
    for n, ref in enumerate((a, b, c, d)):
        out_ref[n * rows : n * rows + rows, :] = ref[...]


def pack_passed(arrived, after):
    rows = arrived[0].shape[0] // 2
    return pl.pallas_call(
        pass_kernel,
        grid=(1,),
        in_specs=[pl.BlockSpec((rows, WIDTH), lambda i: (1, 0))] * NZ + [IN_HBM],
        out_specs=pl.BlockSpec((NZ * rows, WIDTH), lambda i: (0, 0)),
        out_shape=jax.ShapeDtypeStruct((NZ * rows, WIDTH), jnp.bfloat16),
        cost_estimate=pl.CostEstimate(flops=0, bytes_accessed=2 * 2**20, transcendentals=0),
    )(*arrived, after)


def select_kernel(picks, *refs):
    sources, outs = refs[:NX], refs[NX:]
    for dz, out in enumerate(outs):
        for dc in range(NC):
            for s in range(NX):
                for k in range(CAP):
                    block = picks[k * NZ * NC + dz * NC + dc, s]
                    at = pl.ds(pl.multiple_of(block * 2 * THIN, 2 * THIN), 2 * THIN)
                    to = ((dc * NX + s) * CAP + k) * 2 * THIN
                    out[to : to + 2 * THIN, :] = sources[s][at, :]


def select(picks, sources):
    shape = jax.ShapeDtypeStruct((NC * NX * CAP * 2 * THIN, WIDTH), jnp.bfloat16)
    whole = lambda a: pl.BlockSpec(a.shape, lambda i, *_: (0, 0))
    return pl.pallas_call(
        select_kernel,
        grid_spec=pltpu.PrefetchScalarGridSpec(
            num_scalar_prefetch=1,
            grid=(1,),
            in_specs=[whole(s) for s in sources],
            out_specs=[whole(shape)] * NZ,
        ),
        out_shape=[shape] * NZ,
        compiler_params=pltpu.CompilerParams(vmem_limit_bytes=VMEM_LIMIT),
        cost_estimate=pl.CostEstimate(flops=0, bytes_accessed=4 * 2**20, transcendentals=0),
    )(picks, *sources)


TILES = 4


def project_kernel(scalars, *refs):
    fast, slow, weight, w_one, w_two, w_swap, out_ref, a_vm, w_vm, sems = (
        refs[:4],
        refs[4:8],
        *refs[8:],
    )
    t, h = scalars[0], scalars[1]
    core = t & 1
    step = pl.program_id(0)
    rows, cols = a_vm.shape[0], w_vm.shape[2]
    gets_fast = (h >> 1) == 1 - core

    def part_copies(refs):
        return [
            pltpu.make_async_copy(
                ref, a_vm.at[:, pl.ds(e * WIDTH, WIDTH)], sems.at[TILES, e]
            )
            for e, ref in enumerate(refs)
        ]

    def weight_copies(tile, direct):
        per_half = TILES // NC
        at = pl.ds((tile % per_half) * cols, cols)
        span = lambda n, count=1: pl.ds(n * WIDTH, count * WIDTH)
        to = w_vm.at[tile]
        pairs = [(weight.at[:, pl.ds(tile * cols, cols)], to.at[span(0)])]
        if direct:
            pairs += [
                (w_one.at[:, at], to.at[span(1)]),
                (w_two.at[span(0), at], to.at[span(3)]),
                (w_two.at[span(1), at], to.at[span(2)]),
            ]
        else:
            pairs += [
                (w_swap.at[span(0), at], to.at[span(1)]),
                (w_swap.at[span(1), at], to.at[span(3)]),
                (w_swap.at[span(2), at], to.at[span(2)]),
            ]
        return [pltpu.make_async_copy(a, b, sems.at[tile, n]) for n, (a, b) in enumerate(pairs)]

    @pl.when(step == 0)
    def _():
        @pl.when(gets_fast)
        def _():
            for copy in part_copies(fast):
                copy.start()

        @pl.when(jnp.logical_not(gets_fast))
        def _():
            for copy in part_copies(slow):
                copy.start()

        for tile in range(TILES):
            half = tile // (TILES // NC)
            for direct in (True, False):

                @pl.when((core == half) == direct)
                def _(tile=tile, direct=direct):
                    for copy in weight_copies(tile, direct):
                        copy.start()

        for copy in part_copies(fast):
            copy.wait()

    for tile in range(TILES):

        @pl.when(step == tile)
        def _(tile=tile):
            for copy in weight_copies(tile, True):
                copy.wait()

    out_ref[...] = jnp.dot(
        a_vm[...], w_vm[step], preferred_element_type=jnp.float32
    ).astype(jnp.bfloat16)


def project(scalars, fast, slow, weight, w_one, w_two, w_swap):
    anywhere = IN_HBM
    rows, width = CHUNK * BLK, weight.shape[1]
    depth = NHEAD * WIDTH
    inputs = (*fast, *slow, weight, w_one, w_two, w_swap)
    return pl.pallas_call(
        project_kernel,
        grid_spec=pltpu.PrefetchScalarGridSpec(
            num_scalar_prefetch=1,
            grid=(TILES,),
            in_specs=[anywhere] * len(inputs),
            out_specs=pl.BlockSpec((rows, width // TILES), lambda i, s: (0, i)),
            scratch_shapes=[
                pltpu.VMEM((rows, depth), jnp.bfloat16),
                pltpu.VMEM((TILES, depth, width // TILES), jnp.bfloat16),
                pltpu.SemaphoreType.DMA((TILES + 1, NHEAD)),
            ],
        ),
        out_shape=jax.ShapeDtypeStruct((rows, width), jnp.bfloat16),
        compiler_params=pltpu.CompilerParams(vmem_limit_bytes=VMEM_LIMIT),
        cost_estimate=pl.CostEstimate(
            flops=2 * rows * depth * width, bytes_accessed=10 * 2**20, transcendentals=0
        ),
    )(scalars, *inputs)


def per_device(query, keys, values, out_weight, near_list, far_list, stride_table):
    t = lax.axis_index("tm")
    h = lax.axis_index("head")
    core = t % NC
    coords = [(zz, xx, cc) for zz in range(NZ) for xx in range(NX) for cc in range(NC)]
    swap = [(i, i ^ 1) for i in range(NTM)]
    across = [(i, i + 1) for i in range(1, NTM - 1, 2)]
    across = across + [(j, i) for i, j in across]
    place = jnp.stack([t, h]).astype(jnp.int32)

    def thin(a):
        return a.reshape(BLOCKS, THIN, MINSTRIDE, WIDTH)[:, :, 0]

    thinned = jnp.concatenate([thin(keys), thin(values)], axis=1).reshape(-1, WIDTH)
    along_x = [
        lax.ppermute(
            thinned, "tm", [(tm_index(*p), tm_index(p[0], p[1] + d, p[2])) for p in coords]
        )
        for d in range(1, NX)
    ]

    fast_part, slow_part = pack_halos(place, keys, values, thinned)
    halo_fast = lax.ppermute(fast_part, "tm", swap)
    halo_slow = lax.ppermute(slow_part, "tm", across)

    cols = out_weight.shape[1] // NC
    half = lax.dynamic_slice_in_dim(out_weight, core * cols, cols, 1)
    half, *along_x = lax.optimization_barrier((half, *along_x))
    w_one = lax.ppermute(half, "head", [(g, g ^ 1) for g in range(NHEAD)])

    picks, table = index_work(place, stride_table, far_list, near_list)

    packs = select(picks, [thinned] + along_x)
    arrived = [packs[0]]
    for d in range(1, NZ):
        pairs = [(tm_index(*p), tm_index(p[0] + d, p[1], p[2])) for p in coords]
        arrived.append(lax.ppermute(packs[d], "tm", pairs))
    w_two = lax.ppermute(
        jnp.concatenate([half, w_one], axis=0), "head", [(g, g ^ 3) for g in range(NHEAD)]
    )
    near_fast = attend(table, query, keys, values, halo_fast, None, FAST_FIRST, 2)
    halo_slow, near_fast = lax.optimization_barrier((halo_slow, near_fast))
    near_slow = attend(table, query, keys, values, halo_slow, None, SLOW_FIRST, 2)
    passed = lax.ppermute(pack_passed(arrived, near_slow[1]), "tm", swap)
    far = [*arrived, passed]
    w_swap = lax.ppermute(jnp.concatenate([w_one, w_two], axis=0), "tm", swap)
    first_fast, last_fast = merge_far(table, query, near_fast, far, FAST_FIRST, w_two)
    near_slow, first_fast = lax.optimization_barrier((near_slow, first_fast))
    first_slow, last_slow = merge_far(table, query, near_slow, far, SLOW_FIRST, w_swap)

    def exchange(chunk, e, fast):
        pairs = []
        for i in range(NTM):
            frame = (1 - i % NC) if fast else i % NC
            for g in range(NHEAD):
                if (e >= 2) == (g // 2 != frame):
                    pairs.append((i * NHEAD + g, i * NHEAD + (g ^ e)))
        return lax.ppermute(chunk, ("tm", "head"), pairs)

    fast = [last_fast, *(exchange(first_fast, e, True) for e in (1, 2)), exchange(last_fast, 3, True)]
    slow = [
        last_slow,
        *(exchange(first_slow, e, False) for e in (1, 2)),
        exchange(last_slow, 3, False),
    ]
    return project(place, fast, slow, out_weight, w_one, w_two, w_swap)


def solution(mesh):
    placed = (
        P("tm", "head"),
        P("tm", "head"),
        P("tm", "head"),
        P("head", None),
        P("tm", None),
        P(),
        P(),
    )
    return jax.shard_map(
        per_device, mesh=mesh, in_specs=placed, out_specs=P(("tm", "head"), None), check_vma=False
    )
```

```python
import functools
import math

import jax
import jax.numpy as jnp
from jax import lax
from jax.experimental import pallas as pl
from jax.experimental.pallas import tpu as pltpu
from jax.sharding import PartitionSpec as P

HD = 128
BLK = 128
FRAME_BLK = 12
KNEAR = 16
KFAR = 16
CAP = 6
MINSTRIDE = 16
THIN = BLK // MINSTRIDE
HEADS = 3
WIDTH = HEADS * HD
BLOCKS = 24
NX, NZ, NC = 4, 4, 2
NTM = NX * NZ * NC
NHEAD = 4
CHUNK = BLOCKS // NHEAD
FAR_ROWS = NTM * CAP * 2 * THIN
FRAME = FRAME_BLK * BLK
LOG2_SCALE = math.log2(math.e) / math.sqrt(HD)
NT = (((1,), (1,)), ((), ()))
VMEM_LIMIT = 56 * 2**20
UNROLL = 3
SLOT, STRIDE, ORDER = KNEAR, KNEAR + KFAR, BLOCKS
FAST_FIRST, FAST_LAST, SLOW_FIRST, SLOW_LAST = range(4)
IN_HBM = pl.BlockSpec(memory_space=pltpu.HBM)
ANYWHERE = pl.BlockSpec(memory_space=pl.ANY)
IN_VMEM = pl.BlockSpec(memory_space=pltpu.VMEM)


def tm_index(z, x, c):
    return (z % NZ) * NX * NC + (x % NX) * NC + c


def load_far(far_refs, far_vm, sems, first_sem):
    part = NX * CAP * 2 * THIN
    copies = []
    for n, ref in enumerate(far_refs):
        rows = part if n < NZ else NZ * part
        copies.append(
            pltpu.make_async_copy(
                ref.at[pl.ds(0, rows)], far_vm.at[pl.ds(n * part, rows)], sems.at[first_sem + n]
            )
        )
    return copies


def far_block(far_vm, table, block):
    tiles = [
        far_vm[
            pl.ds(pl.multiple_of(table[block, SLOT + j] * 2 * THIN, 2 * THIN), 2 * THIN), :
        ].astype(jnp.float32)
        for j in range(KFAR)
    ]
    keys = jnp.concatenate([t[:THIN] for t in tiles], axis=0).astype(jnp.bfloat16)
    values = jnp.concatenate([t[THIN:] for t in tiles], axis=0).astype(jnp.bfloat16)
    lane = lax.broadcasted_iota(jnp.int32, (1, BLK), 1)
    stride = jnp.zeros((1, BLK), jnp.int32)
    for j in range(KFAR):
        stride = jnp.where(lane // THIN == j, table[block, STRIDE + j], stride)
    used = (((lane % THIN) * MINSTRIDE) & (stride - 1)) == 0
    return keys, values, used


def with_ones(values):
    return jnp.concatenate([values, jnp.ones((values.shape[0], HD), jnp.bfloat16)], axis=1)


def attend_kernel(table, q_ref, k_ref, v_ref, halo_ref, *rest, chunk, with_far, ordering):
    rest = rest[ordering:]
    if with_far:
        far_refs, (out_ref, k_vm, v_vm, s_vm, far_vm, sems) = rest[:5], rest[5:]
    else:
        near_ref, level_ref, k_vm, v_vm, s_vm, sems = rest
    step = pl.program_id(0)
    own = BLOCKS * BLK
    halo = pl.ds(own, FRAME)
    key_copies = [
        pltpu.make_async_copy(k_ref, k_vm.at[pl.ds(0, own)], sems.at[0]),
        pltpu.make_async_copy(halo_ref.at[pl.ds(0, FRAME)], k_vm.at[halo], sems.at[1]),
    ]
    value_copies = [
        pltpu.make_async_copy(v_ref, v_vm.at[pl.ds(0, own)], sems.at[2]),
        pltpu.make_async_copy(halo_ref.at[pl.ds(FRAME, FRAME)], v_vm.at[halo], sems.at[3]),
    ]
    if with_far:
        key_copies += load_far(far_refs, far_vm, sems, 4)

    @pl.when(step == 0)
    def _():
        for copy in key_copies + value_copies:
            copy.start()
        for copy in key_copies:
            copy.wait()

    first = table[ORDER, chunk + step] * CHUNK

    def prepare(unit):
        block = first + unit
        offsets = [pl.multiple_of(table[block, j] * BLK, BLK) for j in range(KNEAR)]
        far = far_block(far_vm, table, block) if with_far else None
        return offsets, far, pl.ds(pl.multiple_of(unit * BLK, BLK), BLK)

    count = KNEAR + (1 if with_far else 0)

    def score_pair(prepared, head, j):
        offsets, far, rows = prepared
        cols = slice(head * HD, head * HD + HD)
        query = q_ref[rows, cols]
        if j < KNEAR:
            keys = jnp.concatenate([k_vm[pl.ds(o, BLK), cols] for o in offsets[j : j + 2]], axis=0)
            both = lax.dot_general(query, keys, NT, preferred_element_type=jnp.float32)
            return [both[:, :BLK], both[:, BLK:]]
        last = lax.dot_general(query, far[0][:, cols], NT, preferred_element_type=jnp.float32)
        return [jnp.where(far[2], last, -1e30)]

    def peak_of(scores):
        top = functools.reduce(jnp.maximum, scores)
        return jnp.max(top, axis=1, keepdims=True) * LOG2_SCALE

    def add_pair(acc, prepared, head, scores, peak, j):
        offsets, far, _ = prepared
        cols = slice(head * HD, head * HD + HD)
        some = range(j, min(j + 2, count))
        weights = jnp.concatenate(
            [jnp.exp2(scores[i] * LOG2_SCALE - peak).astype(jnp.bfloat16) for i in some], axis=1
        )
        values = jnp.concatenate(
            [v_vm[pl.ds(offsets[i], BLK), cols] if i < KNEAR else far[1][:, cols] for i in some],
            axis=0,
        )
        part = jnp.dot(weights, with_ones(values), preferred_element_type=jnp.float32)
        return part if acc is None else acc + part

    def store(prepared, head, peak, acc):
        rows = prepared[2]
        cols = slice(head * HD, head * HD + HD)
        if with_far:
            out_ref[rows, cols] = (acc[:, :HD] / acc[:, HD:]).astype(jnp.bfloat16)
        else:
            near_ref[rows, cols] = (acc[:, :HD] / acc[:, HD:]).astype(jnp.bfloat16)
            level_ref[rows, cols] = peak + jnp.log2(acc[:, HD:])

    def scores_of(prepared, head):
        scores = []
        for j in range(0, count, 2):
            scores += score_pair(prepared, head, j)
        return scores

    def overlap(fresh, pending):
        prepared, head, scores = pending
        peak = peak_of(scores)
        following, acc = [], None
        for j in range(0, count, 2):
            following += score_pair(*fresh, j)
            acc = add_pair(acc, prepared, head, scores, peak, j)
        store(prepared, head, peak, acc)
        return following

    def hold(scores):
        for i, some in enumerate(scores):
            s_vm[:, i * BLK : i * BLK + BLK] = some

    hold(scores_of(prepare(0), 0))

    @pl.when(step == 0)
    def _():
        for copy in value_copies:
            copy.wait()

    units = CHUNK // UNROLL

    def body(i, _):
        pending = None
        scores = [s_vm[:, n * BLK : n * BLK + BLK] for n in range(count)]
        for u in range(UNROLL):
            unit = i * UNROLL + u
            prepared = prepare(unit)
            for head in range(HEADS):
                if head or u:
                    scores = overlap((prepared, head), pending)
                pending = prepared, head, scores
        after = prepare(jnp.minimum(i * UNROLL + UNROLL, CHUNK - 1))
        hold(overlap((after, 0), pending))
        return 0

    lax.fori_loop(0, units, body, 0)


def attend(table, query, keys, values, halo, far, chunk, chunks, after=()):
    with_far = far is not None
    spot = lambda i, s: (s[ORDER, chunk + i], 0)
    same = lambda i, s: (i, 0)
    rows = CHUNK * BLK
    scratch = [pltpu.VMEM((BLOCKS * BLK + FRAME, WIDTH), jnp.bfloat16) for _ in range(2)]
    scratch.append(pltpu.VMEM((BLK, (KNEAR + 1) * BLK), jnp.float32))
    if with_far:
        scratch.append(pltpu.VMEM((FAR_ROWS, WIDTH), jnp.bfloat16))
        out_shape = jax.ShapeDtypeStruct((chunks * rows, WIDTH), jnp.bfloat16)
        out_specs = pl.BlockSpec((rows, WIDTH), same)
    else:
        out_shape = [
            jax.ShapeDtypeStruct((chunks * rows, WIDTH), kind)
            for kind in (jnp.bfloat16, jnp.float32)
        ]
        out_specs = [pl.BlockSpec((rows, WIDTH), same)] * 2
    scratch.append(pltpu.SemaphoreType.DMA((9,)))
    extra = tuple(far) if with_far else ()
    return pl.pallas_call(
        functools.partial(
            attend_kernel, chunk=chunk, with_far=with_far, ordering=len(after)
        ),
        grid_spec=pltpu.PrefetchScalarGridSpec(
            num_scalar_prefetch=1,
            grid=(chunks,),
            in_specs=[pl.BlockSpec((rows, WIDTH), spot)] + [IN_HBM] * 3 + [ANYWHERE] * len(after + extra),
            out_specs=out_specs,
            scratch_shapes=scratch,
        ),
        out_shape=out_shape,
        compiler_params=pltpu.CompilerParams(vmem_limit_bytes=VMEM_LIMIT),
        cost_estimate=pl.CostEstimate(
            flops=chunks * CHUNK * HEADS * 17 * 4 * BLK * BLK * HD * 3,
            bytes_accessed=8 * 2**20,
            transcendentals=0,
        ),
    )(table, query, keys, values, halo, *after, *extra)


def merge_kernel(table, q_ref, near_ref, level_ref, *rest, chunk):
    far_refs, (_, first_ref, last_ref, out_vm, far_vm, sems) = rest[:5], rest[5:]
    step = pl.program_id(0)

    @pl.when(step == 0)
    def _():
        copies = load_far(far_refs, far_vm, sems, 0)
        for copy in copies:
            copy.start()
        for copy in copies:
            copy.wait()

    first = table[ORDER, chunk + step] * CHUNK
    spot = {
        (unit, head): (
            slice(unit * BLK, unit * BLK + BLK),
            slice(head * HD, head * HD + HD),
        )
        for unit in range(CHUNK)
        for head in range(HEADS)
    }
    far = [far_block(far_vm, table, first + unit) for unit in range(CHUNK)]
    scores, peaks, sums = {}, {}, {}
    for p, (rows, cols) in spot.items():
        keys, _, used = far[p[0]]
        some = lax.dot_general(
            q_ref[rows, cols], keys[:, cols], NT, preferred_element_type=jnp.float32
        )
        scores[p] = jnp.where(used, some, -1e30) * LOG2_SCALE
    for p, (rows, cols) in spot.items():
        peaks[p] = jnp.maximum(jnp.max(scores[p], axis=1, keepdims=True), level_ref[rows, cols])
    for p, (rows, cols) in spot.items():
        weights = jnp.exp2(scores[p] - peaks[p]).astype(jnp.bfloat16)
        values = far[p[0]][1][:, cols]
        sums[p] = jnp.dot(weights, with_ones(values), preferred_element_type=jnp.float32)
    for p, (rows, cols) in spot.items():
        share = jnp.exp2(level_ref[rows, cols] - peaks[p])
        total = share + sums[p][:, HD:]
        mixed = near_ref[rows, cols].astype(jnp.float32) * share + sums[p][:, :HD]
        out_vm[step, rows, cols] = (mixed / total).astype(jnp.bfloat16)

    outs = [
        pltpu.make_async_copy(out_vm.at[n], ref, sems.at[5 + n])
        for n, ref in enumerate((first_ref, last_ref))
    ]

    @pl.when(step == 0)
    def _():
        outs[0].start()

    @pl.when(step == 1)
    def _():
        outs[1].start()
        for copy in outs:
            copy.wait()


def merge_far(table, query, state, far, chunk, after):
    rows = CHUNK * BLK
    return pl.pallas_call(
        functools.partial(merge_kernel, chunk=chunk),
        grid_spec=pltpu.PrefetchScalarGridSpec(
            num_scalar_prefetch=1,
            grid=(2,),
            in_specs=[pl.BlockSpec((rows, WIDTH), lambda i, s: (s[ORDER, chunk + i], 0))]
            + [pl.BlockSpec((rows, WIDTH), lambda i, s: (i, 0))] * 2
            + [ANYWHERE] * 6,
            out_specs=[IN_HBM] * 2,
            scratch_shapes=[
                pltpu.VMEM((2, rows, WIDTH), jnp.bfloat16),
                pltpu.VMEM((FAR_ROWS, WIDTH), jnp.bfloat16),
                pltpu.SemaphoreType.DMA((7,)),
            ],
        ),
        out_shape=[jax.ShapeDtypeStruct((rows, WIDTH), jnp.bfloat16)] * 2,
        compiler_params=pltpu.CompilerParams(vmem_limit_bytes=VMEM_LIMIT),
        cost_estimate=pl.CostEstimate(
            flops=2 * CHUNK * HEADS * 4 * BLK * BLK * HD * 6,
            bytes_accessed=8 * 2**20,
            transcendentals=0,
        ),
    )(table, query, *state, *far, after)


def index_kernel(scalars, steps, far_ref, near_ref, picks_ref, table_ref):
    t = scalars[0]
    core, x, z = t & 1, (t >> 1) & 3, t >> 3
    lane = lax.broadcasted_iota(jnp.int32, (1, BLK), 1)
    group = (lane * 2731) >> 16
    within = lane - group * BLOCKS
    valid = lane < NX * BLOCKS

    source = ((z * NX + ((x - group) & 3)) * NC + core) * BLOCKS + within
    source = jnp.where(valid, source, -1)
    present = []
    for dz in range(NZ):
        for dc in range(NC):
            receiver = (((z + dz) & 3) * NX + x) * NC + (core ^ dc)
            listed = far_ref[pl.ds(pl.multiple_of(receiver * BLOCKS, 8), BLOCKS), :]
            found = jnp.zeros((BLOCKS, BLK), jnp.float32)
            for j in range(KFAR):
                found = jnp.where(listed[:, j : j + 1] == source, 1.0, found)
            present.append(jnp.max(found, axis=0, keepdims=True))

    mine = far_ref[pl.ds(pl.multiple_of(t * BLOCKS, 8), BLOCKS), :]
    ids = [jnp.where(valid, row * NX * BLOCKS + lane, -1) for row in range(NTM // NX)]
    found = [jnp.zeros((BLOCKS, BLK), jnp.float32) for _ in ids]
    for j in range(KFAR):
        column = jnp.broadcast_to(mine[:, j : j + 1], (BLOCKS, BLK))
        found = [jnp.where(column == i, 1.0, f) for i, f in zip(ids, found)]
    present += [jnp.max(f, axis=0, keepdims=True) for f in found]
    present = jnp.concatenate(present, axis=0)

    a = lax.broadcasted_iota(jnp.int32, (BLK, BLK), 0)
    b = lax.broadcasted_iota(jnp.int32, (BLK, BLK), 1)
    group_a, group_b = (a * 2731) >> 16, (b * 2731) >> 16
    before = jnp.where((group_a == group_b) & (a < b), 1.0, 0.0).astype(jnp.bfloat16)
    rank = jnp.dot(present.astype(jnp.bfloat16), before, preferred_element_type=jnp.float32)

    receivers = NZ * NC
    chosen = [
        jnp.where((present[:receivers] > 0) & (rank[:receivers] == k), within.astype(jnp.float32), 0.0)
        for k in range(CAP)
    ]
    gather = jnp.where(group_a == b, 1.0, 0.0).astype(jnp.bfloat16)
    picks = jnp.dot(
        jnp.concatenate(chosen, axis=0).astype(jnp.bfloat16),
        gather,
        preferred_element_type=jnp.float32,
    )
    picks_ref[...] = picks.astype(jnp.int32)

    lies = []
    for row in range(NTM // NX):
        device = row * NX + group
        dz = (z - (device >> 3)) & 3
        dx = (x - (device >> 1)) & 3
        dc = core ^ (device & 1)
        start = ((dc * NZ + dz) * NX + dx) * CAP
        lies.append(start.astype(jnp.float32) + rank[receivers + row : receivers + row + 1])
    entry = lax.broadcasted_iota(jnp.int32, (BLOCKS, KFAR), 1)
    slots = jnp.zeros((BLOCKS, KFAR), jnp.float32)
    for j in range(KFAR):
        column = jnp.broadcast_to(mine[:, j : j + 1], (BLOCKS, BLK))
        at = jnp.zeros((BLOCKS, BLK), jnp.float32)
        for i, where in zip(ids, lies):
            at = jnp.where(column == i, where, at)
        slots = jnp.where(entry == j, jnp.sum(at, axis=1, keepdims=True), slots)

    row = lax.broadcasted_iota(jnp.int32, (BLOCKS, KFAR), 0)
    frame = t * (BLOCKS // FRAME_BLK) + jnp.where(row >= FRAME_BLK, 1, 0)
    distance = jnp.abs(frame - ((mine * 5462) >> 16))
    strides = jnp.zeros((BLOCKS, KFAR), jnp.int32)
    for d in range(steps.shape[0]):
        strides = jnp.where(distance == d, steps[d], strides)

    local = near_ref[...] - t * BLOCKS
    local = jnp.where(local < 0, local + FRAME_BLK + BLOCKS, local)
    rest = jnp.zeros((BLOCKS, BLK - KNEAR - 2 * KFAR), jnp.int32)
    table_ref[:BLOCKS, :] = jnp.concatenate(
        [local, slots.astype(jnp.int32), strides, rest], axis=1
    )

    h = scalars[1]
    order = jnp.zeros((8, BLK), jnp.int32)
    column = lax.broadcasted_iota(jnp.int32, (8, BLK), 1)
    for at, half in ((FAST_FIRST, 1 - core), (SLOW_FIRST, core)):
        inside = (h >> 1) == half
        order = jnp.where(column == at, jnp.where(inside, h ^ 1, h ^ 2), order)
        order = jnp.where(column == at + 1, jnp.where(inside, h, h ^ 3), order)
    table_ref[BLOCKS:, :] = order


def index_work(scalars, steps, far_list, near_list):
    whole = lambda shape: pl.BlockSpec(shape, lambda i, *_: (0, 0))
    shapes = [(NZ * NC * CAP, BLK), (BLOCKS + 8, BLK)]
    return pl.pallas_call(
        index_kernel,
        grid_spec=pltpu.PrefetchScalarGridSpec(
            num_scalar_prefetch=2,
            grid=(1,),
            in_specs=[whole(far_list.shape), whole(near_list.shape)],
            out_specs=[whole(shape) for shape in shapes],
        ),
        out_shape=[jax.ShapeDtypeStruct(shape, jnp.int32) for shape in shapes],
        cost_estimate=pl.CostEstimate(flops=2**20, bytes_accessed=2**22, transcendentals=0),
    )(scalars, steps, far_list, near_list)


def halo_kernel(scalars, k_fast, v_fast, k_slow, v_slow, after, fast_ref, slow_ref):
    fast_ref[0] = k_fast[...]
    fast_ref[1] = v_fast[...]
    slow_ref[0] = k_slow[...]
    slow_ref[1] = v_slow[...]


def pack_halos(scalars, keys, values, after):
    parts = 4
    rows = FRAME // parts
    fast = pl.BlockSpec((rows, WIDTH), lambda i, s: ((1 - (s[0] & 1)) * parts + i, 0))
    slow = pl.BlockSpec((rows, WIDTH), lambda i, s: ((s[0] & 1) * parts + i, 0))
    shape = jax.ShapeDtypeStruct((2, FRAME, WIDTH), jnp.bfloat16)
    outs = pl.pallas_call(
        halo_kernel,
        grid_spec=pltpu.PrefetchScalarGridSpec(
            num_scalar_prefetch=1,
            grid=(parts,),
            in_specs=[fast, fast, slow, slow, ANYWHERE],
            out_specs=[pl.BlockSpec((2, rows, WIDTH), lambda i, s: (0, i, 0))] * 2,
        ),
        out_shape=[shape] * 2,
        cost_estimate=pl.CostEstimate(flops=0, bytes_accessed=10 * 2**20, transcendentals=0),
    )(scalars, keys, values, keys, values, after)
    return [out.reshape(2 * FRAME, WIDTH) for out in outs]


def pass_kernel(a, b, c, d, after, out_ref):
    rows = a.shape[0]
    for n, ref in enumerate((a, b, c, d)):
        out_ref[n * rows : n * rows + rows, :] = ref[...]


def pack_passed(arrived, after):
    rows = arrived[0].shape[0] // 2
    return pl.pallas_call(
        pass_kernel,
        grid=(1,),
        in_specs=[pl.BlockSpec((rows, WIDTH), lambda i: (1, 0))] * NZ + [ANYWHERE],
        out_specs=pl.BlockSpec((NZ * rows, WIDTH), lambda i: (0, 0)),
        out_shape=jax.ShapeDtypeStruct((NZ * rows, WIDTH), jnp.bfloat16),
        cost_estimate=pl.CostEstimate(flops=0, bytes_accessed=2 * 2**20, transcendentals=0),
    )(*arrived, after)


def select_kernel(picks, *refs):
    sources, outs = refs[:NX], refs[NX + 1 :]
    for dz, out in enumerate(outs):
        for dc in range(NC):
            for s in range(NX):
                for k in range(CAP):
                    block = picks[k * NZ * NC + dz * NC + dc, s]
                    at = pl.ds(pl.multiple_of(block * 2 * THIN, 2 * THIN), 2 * THIN)
                    to = ((dc * NX + s) * CAP + k) * 2 * THIN
                    out[to : to + 2 * THIN, :] = sources[s][at, :]


def select(picks, sources, after):
    shape = jax.ShapeDtypeStruct((NC * NX * CAP * 2 * THIN, WIDTH), jnp.bfloat16)
    whole = lambda a: pl.BlockSpec(a.shape, lambda i, *_: (0, 0))
    return pl.pallas_call(
        select_kernel,
        grid_spec=pltpu.PrefetchScalarGridSpec(
            num_scalar_prefetch=1,
            grid=(1,),
            in_specs=[whole(s) for s in sources] + [ANYWHERE],
            out_specs=[whole(shape)] * NZ,
        ),
        out_shape=[shape] * NZ,
        compiler_params=pltpu.CompilerParams(vmem_limit_bytes=VMEM_LIMIT),
        cost_estimate=pl.CostEstimate(flops=0, bytes_accessed=4 * 2**20, transcendentals=0),
    )(picks, *sources, after)


ROW_TILE = 256


def project_kernel(scalars, *refs, wanted_fast, held):
    parts, (weight, w_one, w_two, w_swap) = refs[:4], refs[4:8]
    out_ref, out_vm, sems = refs[8 + held :]
    core, h = scalars[0] & 1, scalars[1]
    gets_fast = (h >> 1) == 1 - core
    tiles = out_vm.shape[0] // ROW_TILE
    width = out_vm.shape[1] // NC

    def copy_of(i):
        rows = pl.ds(pl.multiple_of(i * ROW_TILE, ROW_TILE), ROW_TILE)
        return pltpu.make_async_copy(out_vm.at[rows], out_ref.at[rows], sems.at[i])

    def group(n):
        return pl.ds(n * WIDTH, WIDTH)

    for mine in range(NC):

        @pl.when((core == mine) & (gets_fast == wanted_fast))
        def _(mine=mine):
            def step(i, _):
                rows = pl.ds(pl.multiple_of(i * ROW_TILE, ROW_TILE), ROW_TILE)
                attended = jnp.concatenate([part[rows, :] for part in parts], axis=1)
                for half in range(NC):
                    cols = pl.ds(half * width, width)
                    if half == mine:
                        others = w_one[...], w_two[group(1), :], w_two[group(0), :]
                    else:
                        others = w_swap[group(0), :], w_swap[group(2), :], w_swap[group(1), :]
                    out_vm[rows, cols] = jnp.dot(
                        attended,
                        jnp.concatenate([weight[:, cols], *others], axis=0),
                        preferred_element_type=jnp.float32,
                    ).astype(jnp.bfloat16)
                copy_of(i).start()
                return 0

            lax.fori_loop(0, tiles, step, 0)
            for i in range(tiles):
                copy_of(i).wait()


def project(scalars, parts, weights, wanted_fast, held=None):
    rows, width = CHUNK * BLK, weights[0].shape[1]
    inputs = (*parts, *weights)
    extra = () if held is None else (held,)
    return pl.pallas_call(
        functools.partial(project_kernel, wanted_fast=wanted_fast, held=len(extra)),
        grid_spec=pltpu.PrefetchScalarGridSpec(
            num_scalar_prefetch=1,
            grid=(1,),
            in_specs=[IN_VMEM] * len(inputs) + [IN_HBM] * len(extra),
            out_specs=IN_HBM,
            scratch_shapes=[
                pltpu.VMEM((rows, width), jnp.bfloat16),
                pltpu.SemaphoreType.DMA((rows // ROW_TILE,)),
            ],
        ),
        out_shape=jax.ShapeDtypeStruct((rows, width), jnp.bfloat16),
        input_output_aliases={} if held is None else {1 + len(inputs): 0},
        compiler_params=pltpu.CompilerParams(vmem_limit_bytes=24 * 2**20),
        cost_estimate=pl.CostEstimate(
            flops=2 * rows * NHEAD * WIDTH * width, bytes_accessed=10 * 2**20, transcendentals=0
        ),
    )(scalars, *inputs, *extra)


def per_device(query, keys, values, out_weight, near_list, far_list, stride_table):
    t = lax.axis_index("tm")
    h = lax.axis_index("head")
    coords = [(zz, xx, cc) for zz in range(NZ) for xx in range(NX) for cc in range(NC)]
    swap = [(i, i ^ 1) for i in range(NTM)]
    across = [(i, i + 1) for i in range(1, NTM - 1, 2)]
    across = across + [(j, i) for i, j in across]
    place = jnp.stack([t, h]).astype(jnp.int32)

    def thin(a):
        return a.reshape(BLOCKS, THIN, MINSTRIDE, WIDTH)[:, :, 0]

    thinned = jnp.concatenate([thin(keys), thin(values)], axis=1).reshape(-1, WIDTH)
    along_x = [
        lax.ppermute(
            thinned, "tm", [(tm_index(*p), tm_index(p[0], p[1] + d, p[2])) for p in coords]
        )
        for d in range(1, NX)
    ]

    fast_part, slow_part = pack_halos(place, keys, values, thinned)
    halo_fast = lax.ppermute(fast_part, "tm", swap)
    picks, table = index_work(place, stride_table, far_list, near_list)
    slow_part, table, *along_x = lax.optimization_barrier((slow_part, table, *along_x))
    halo_slow = lax.ppermute(slow_part, "tm", across)

    near_fast = attend(table, query, keys, values, halo_fast, None, FAST_FIRST, 2)
    packs = select(picks, [thinned] + along_x, near_fast[1])
    arrived = [packs[0]]
    for d in range(1, NZ):
        pairs = [(tm_index(*p), tm_index(p[0] + d, p[1], p[2])) for p in coords]
        arrived.append(lax.ppermute(packs[d], "tm", pairs))

    cols = out_weight.shape[1] // NC
    half = lax.dynamic_slice_in_dim(out_weight, (t % NC) * cols, cols, 1)
    half, _ = lax.optimization_barrier((half, table))
    w_one = lax.ppermute(half, "head", [(g, g ^ 1) for g in range(NHEAD)])
    half, w_one, _ = lax.optimization_barrier((half, w_one, packs[0]))
    w_two = lax.ppermute(
        jnp.concatenate([half, w_one], axis=0), "head", [(g, g ^ 3) for g in range(NHEAD)]
    )

    near_slow = attend(
        table, query, keys, values, halo_slow, None, SLOW_FIRST, 2, (packs[0],)
    )
    passed = lax.ppermute(pack_passed(arrived, near_slow[1]), "tm", swap)
    far = [*arrived, passed]
    w_swap = lax.ppermute(jnp.concatenate([w_one, w_two], axis=0), "tm", swap)
    first_fast, last_fast = merge_far(table, query, near_fast, far, FAST_FIRST, near_slow[1])
    near_slow, first_fast = lax.optimization_barrier((near_slow, first_fast))
    first_slow, last_slow = merge_far(table, query, near_slow, far, SLOW_FIRST, w_swap)

    def exchange(chunk, e, fast):
        pairs = []
        for i in range(NTM):
            frame = (1 - i % NC) if fast else i % NC
            for g in range(NHEAD):
                if (e >= 2) == (g // 2 != frame):
                    pairs.append((i * NHEAD + g, i * NHEAD + (g ^ e)))
        return lax.ppermute(chunk, ("tm", "head"), pairs)

    def received(first, last, fast):
        two, one, three = [
            exchange(chunk, e, fast) for e, chunk in ((2, first), (1, first), (3, last))
        ]
        return last, one, two, three

    weights = (out_weight, w_one, w_two, w_swap)
    fast = received(first_fast, last_fast, True)
    slow = received(first_slow, last_slow, False)
    held = project(place, fast, weights, True)
    return project(place, slow, weights, False, held)


def solution(mesh):
    placed = (
        P("tm", "head"),
        P("tm", "head"),
        P("tm", "head"),
        P("head", None),
        P("tm", None),
        P(),
        P(),
    )
    return jax.shard_map(
        per_device, mesh=mesh, in_specs=placed, out_specs=P(("tm", "head"), None), check_vma=False
    )
```

```python
import functools
import math

import jax
import jax.numpy as jnp
from jax import lax
from jax.experimental import pallas as pl
from jax.experimental.pallas import tpu as pltpu
from jax.sharding import PartitionSpec as P

HD = 128
BLK = 128
FRAME_BLK = 12
KNEAR = 16
KFAR = 16
CAP = 6
MINSTRIDE = 16
THIN = BLK // MINSTRIDE
HEADS = 3
WIDTH = HEADS * HD
BLOCKS = 24
NX, NZ, NC = 4, 4, 2
NTM = NX * NZ * NC
NHEAD = 4
CHUNK = BLOCKS // NHEAD
FAR_ROWS = NTM * CAP * 2 * THIN
FRAME = FRAME_BLK * BLK
LOG2_SCALE = math.log2(math.e) / math.sqrt(HD)
NT = (((1,), (1,)), ((), ()))
VMEM_LIMIT = 56 * 2**20
UNROLL = 3
SLOT, STRIDE, ORDER = KNEAR, KNEAR + KFAR, BLOCKS
FAST_FIRST, FAST_LAST, SLOW_FIRST, SLOW_LAST = range(4)
IN_HBM = pl.BlockSpec(memory_space=pltpu.HBM)
ANYWHERE = pl.BlockSpec(memory_space=pl.ANY)
IN_VMEM = pl.BlockSpec(memory_space=pltpu.VMEM)


def tm_index(z, x, c):
    return (z % NZ) * NX * NC + (x % NX) * NC + c


def load_far(far_refs, far_vm, sems, first_sem):
    part = NX * CAP * 2 * THIN
    copies = []
    for n, ref in enumerate(far_refs):
        rows = part if n < NZ else NZ * part
        copies.append(
            pltpu.make_async_copy(
                ref.at[pl.ds(0, rows)], far_vm.at[pl.ds(n * part, rows)], sems.at[first_sem + n]
            )
        )
    return copies


def far_block(far_vm, table, block):
    tiles = [
        far_vm[
            pl.ds(pl.multiple_of(table[block, SLOT + j] * 2 * THIN, 2 * THIN), 2 * THIN), :
        ].astype(jnp.float32)
        for j in range(KFAR)
    ]
    keys = jnp.concatenate([t[:THIN] for t in tiles], axis=0).astype(jnp.bfloat16)
    values = jnp.concatenate([t[THIN:] for t in tiles], axis=0).astype(jnp.bfloat16)
    lane = lax.broadcasted_iota(jnp.int32, (1, BLK), 1)
    stride = jnp.zeros((1, BLK), jnp.int32)
    for j in range(KFAR):
        stride = jnp.where(lane // THIN == j, table[block, STRIDE + j], stride)
    used = (((lane % THIN) * MINSTRIDE) & (stride - 1)) == 0
    return keys, values, used


def with_ones(values):
    return jnp.concatenate([values, jnp.ones((values.shape[0], HD), jnp.bfloat16)], axis=1)


def attend_kernel(table, q_ref, k_ref, v_ref, halo_ref, *rest, chunk, with_far, ordering):
    rest = rest[ordering:]
    if with_far:
        far_refs, (out_ref, k_vm, v_vm, s_vm, far_vm, sems) = rest[:5], rest[5:]
    else:
        near_ref, level_ref, k_vm, v_vm, s_vm, sems = rest
    step = pl.program_id(0)
    own = BLOCKS * BLK
    halo = pl.ds(own, FRAME)
    key_copies = [
        pltpu.make_async_copy(k_ref, k_vm.at[pl.ds(0, own)], sems.at[0]),
        pltpu.make_async_copy(halo_ref.at[pl.ds(0, FRAME)], k_vm.at[halo], sems.at[1]),
    ]
    value_copies = [
        pltpu.make_async_copy(v_ref, v_vm.at[pl.ds(0, own)], sems.at[2]),
        pltpu.make_async_copy(halo_ref.at[pl.ds(FRAME, FRAME)], v_vm.at[halo], sems.at[3]),
    ]
    if with_far:
        key_copies += load_far(far_refs, far_vm, sems, 4)

    @pl.when(step == 0)
    def _():
        for copy in key_copies + value_copies:
            copy.start()
        for copy in key_copies:
            copy.wait()

    first = table[ORDER, chunk + step] * CHUNK

    def prepare(unit):
        block = first + unit
        offsets = [pl.multiple_of(table[block, j] * BLK, BLK) for j in range(KNEAR)]
        far = far_block(far_vm, table, block) if with_far else None
        return offsets, far, pl.ds(pl.multiple_of(unit * BLK, BLK), BLK)

    count = KNEAR + (1 if with_far else 0)

    def score_pair(prepared, head, j):
        offsets, far, rows = prepared
        cols = slice(head * HD, head * HD + HD)
        query = q_ref[rows, cols]
        if j < KNEAR:
            keys = jnp.concatenate([k_vm[pl.ds(o, BLK), cols] for o in offsets[j : j + 2]], axis=0)
            both = lax.dot_general(query, keys, NT, preferred_element_type=jnp.float32)
            return [both[:, :BLK], both[:, BLK:]]
        last = lax.dot_general(query, far[0][:, cols], NT, preferred_element_type=jnp.float32)
        return [jnp.where(far[2], last, -1e30)]

    def peak_of(scores):
        top = functools.reduce(jnp.maximum, scores)
        return jnp.max(top, axis=1, keepdims=True) * LOG2_SCALE

    def add_pair(acc, prepared, head, scores, peak, j):
        offsets, far, _ = prepared
        cols = slice(head * HD, head * HD + HD)
        some = range(j, min(j + 2, count))
        weights = jnp.concatenate(
            [jnp.exp2(scores[i] * LOG2_SCALE - peak).astype(jnp.bfloat16) for i in some], axis=1
        )
        values = jnp.concatenate(
            [v_vm[pl.ds(offsets[i], BLK), cols] if i < KNEAR else far[1][:, cols] for i in some],
            axis=0,
        )
        part = jnp.dot(weights, with_ones(values), preferred_element_type=jnp.float32)
        return part if acc is None else acc + part

    def store(prepared, head, peak, acc):
        rows = prepared[2]
        cols = slice(head * HD, head * HD + HD)
        if with_far:
            out_ref[rows, cols] = (acc[:, :HD] / acc[:, HD:]).astype(jnp.bfloat16)
        else:
            near_ref[rows, cols] = (acc[:, :HD] / acc[:, HD:]).astype(jnp.bfloat16)
            level_ref[rows, cols] = peak + jnp.log2(acc[:, HD:])

    def scores_of(prepared, head):
        scores = []
        for j in range(0, count, 2):
            scores += score_pair(prepared, head, j)
        return scores

    def overlap(fresh, pending):
        prepared, head, scores = pending
        peak = peak_of(scores)
        following, acc = [], None
        for j in range(0, count, 2):
            following += score_pair(*fresh, j)
            acc = add_pair(acc, prepared, head, scores, peak, j)
        store(prepared, head, peak, acc)
        return following

    def hold(scores):
        for i, some in enumerate(scores):
            s_vm[:, i * BLK : i * BLK + BLK] = some

    hold(scores_of(prepare(0), 0))

    @pl.when(step == 0)
    def _():
        for copy in value_copies:
            copy.wait()

    units = CHUNK // UNROLL

    def body(i, _):
        pending = None
        scores = [s_vm[:, n * BLK : n * BLK + BLK] for n in range(count)]
        for u in range(UNROLL):
            unit = i * UNROLL + u
            prepared = prepare(unit)
            for head in range(HEADS):
                if head or u:
                    scores = overlap((prepared, head), pending)
                pending = prepared, head, scores
        after = prepare(jnp.minimum(i * UNROLL + UNROLL, CHUNK - 1))
        hold(overlap((after, 0), pending))
        return 0

    lax.fori_loop(0, units, body, 0)


def attend(table, query, keys, values, halo, far, chunk, chunks, after=()):
    with_far = far is not None
    spot = lambda i, s: (s[ORDER, chunk + i], 0)
    same = lambda i, s: (i, 0)
    rows = CHUNK * BLK
    scratch = [pltpu.VMEM((BLOCKS * BLK + FRAME, WIDTH), jnp.bfloat16) for _ in range(2)]
    scratch.append(pltpu.VMEM((BLK, (KNEAR + 1) * BLK), jnp.float32))
    if with_far:
        scratch.append(pltpu.VMEM((FAR_ROWS, WIDTH), jnp.bfloat16))
        out_shape = jax.ShapeDtypeStruct((chunks * rows, WIDTH), jnp.bfloat16)
        out_specs = pl.BlockSpec((rows, WIDTH), same)
    else:
        out_shape = [
            jax.ShapeDtypeStruct((chunks * rows, WIDTH), kind)
            for kind in (jnp.bfloat16, jnp.float32)
        ]
        out_specs = [pl.BlockSpec((rows, WIDTH), same)] * 2
    scratch.append(pltpu.SemaphoreType.DMA((9,)))
    extra = tuple(far) if with_far else ()
    return pl.pallas_call(
        functools.partial(
            attend_kernel, chunk=chunk, with_far=with_far, ordering=len(after)
        ),
        grid_spec=pltpu.PrefetchScalarGridSpec(
            num_scalar_prefetch=1,
            grid=(chunks,),
            in_specs=[pl.BlockSpec((rows, WIDTH), spot)] + [IN_HBM] * 3 + [ANYWHERE] * len(after + extra),
            out_specs=out_specs,
            scratch_shapes=scratch,
        ),
        out_shape=out_shape,
        compiler_params=pltpu.CompilerParams(vmem_limit_bytes=VMEM_LIMIT),
        cost_estimate=pl.CostEstimate(
            flops=chunks * CHUNK * HEADS * 17 * 4 * BLK * BLK * HD * 3,
            bytes_accessed=8 * 2**20,
            transcendentals=0,
        ),
    )(table, query, keys, values, halo, *after, *extra)


def merge_kernel(table, q_ref, near_ref, level_ref, *rest, chunk):
    far_refs, (_, first_ref, last_ref, out_vm, far_vm, sems) = rest[:5], rest[5:]
    step = pl.program_id(0)

    @pl.when(step == 0)
    def _():
        copies = load_far(far_refs, far_vm, sems, 0)
        for copy in copies:
            copy.start()
        for copy in copies:
            copy.wait()

    first = table[ORDER, chunk + step] * CHUNK
    spot = {
        (unit, head): (
            slice(unit * BLK, unit * BLK + BLK),
            slice(head * HD, head * HD + HD),
        )
        for unit in range(CHUNK)
        for head in range(HEADS)
    }
    far = [far_block(far_vm, table, first + unit) for unit in range(CHUNK)]
    scores, peaks, sums = {}, {}, {}
    for p, (rows, cols) in spot.items():
        keys, _, used = far[p[0]]
        some = lax.dot_general(
            q_ref[rows, cols], keys[:, cols], NT, preferred_element_type=jnp.float32
        )
        scores[p] = jnp.where(used, some, -1e30) * LOG2_SCALE
    for p, (rows, cols) in spot.items():
        peaks[p] = jnp.maximum(jnp.max(scores[p], axis=1, keepdims=True), level_ref[rows, cols])
    for p, (rows, cols) in spot.items():
        weights = jnp.exp2(scores[p] - peaks[p]).astype(jnp.bfloat16)
        values = far[p[0]][1][:, cols]
        sums[p] = jnp.dot(weights, with_ones(values), preferred_element_type=jnp.float32)
    for p, (rows, cols) in spot.items():
        share = jnp.exp2(level_ref[rows, cols] - peaks[p])
        total = share + sums[p][:, HD:]
        mixed = near_ref[rows, cols].astype(jnp.float32) * share + sums[p][:, :HD]
        out_vm[step, rows, cols] = (mixed / total).astype(jnp.bfloat16)

    outs = [
        pltpu.make_async_copy(out_vm.at[n], ref, sems.at[5 + n])
        for n, ref in enumerate((first_ref, last_ref))
    ]

    @pl.when(step == 0)
    def _():
        outs[0].start()

    @pl.when(step == 1)
    def _():
        outs[1].start()
        for copy in outs:
            copy.wait()


def merge_far(table, query, state, far, chunk, after):
    rows = CHUNK * BLK
    return pl.pallas_call(
        functools.partial(merge_kernel, chunk=chunk),
        grid_spec=pltpu.PrefetchScalarGridSpec(
            num_scalar_prefetch=1,
            grid=(2,),
            in_specs=[pl.BlockSpec((rows, WIDTH), lambda i, s: (s[ORDER, chunk + i], 0))]
            + [pl.BlockSpec((rows, WIDTH), lambda i, s: (i, 0))] * 2
            + [ANYWHERE] * 6,
            out_specs=[IN_HBM] * 2,
            scratch_shapes=[
                pltpu.VMEM((2, rows, WIDTH), jnp.bfloat16),
                pltpu.VMEM((FAR_ROWS, WIDTH), jnp.bfloat16),
                pltpu.SemaphoreType.DMA((7,)),
            ],
        ),
        out_shape=[jax.ShapeDtypeStruct((rows, WIDTH), jnp.bfloat16)] * 2,
        compiler_params=pltpu.CompilerParams(vmem_limit_bytes=VMEM_LIMIT),
        cost_estimate=pl.CostEstimate(
            flops=2 * CHUNK * HEADS * 4 * BLK * BLK * HD * 6,
            bytes_accessed=8 * 2**20,
            transcendentals=0,
        ),
    )(table, query, *state, *far, after)


def index_kernel(scalars, steps, far_ref, near_ref, picks_ref, table_ref):
    t = scalars[0]
    core, x, z = t & 1, (t >> 1) & 3, t >> 3
    lane = lax.broadcasted_iota(jnp.int32, (1, BLK), 1)
    group = (lane * 2731) >> 16
    within = lane - group * BLOCKS
    valid = lane < NX * BLOCKS

    source = ((z * NX + ((x - group) & 3)) * NC + core) * BLOCKS + within
    source = jnp.where(valid, source, -1)
    present = []
    for dz in range(NZ):
        for dc in range(NC):
            receiver = (((z + dz) & 3) * NX + x) * NC + (core ^ dc)
            listed = far_ref[pl.ds(pl.multiple_of(receiver * BLOCKS, 8), BLOCKS), :]
            found = jnp.zeros((BLOCKS, BLK), jnp.float32)
            for j in range(KFAR):
                found = jnp.where(listed[:, j : j + 1] == source, 1.0, found)
            present.append(jnp.max(found, axis=0, keepdims=True))

    mine = far_ref[pl.ds(pl.multiple_of(t * BLOCKS, 8), BLOCKS), :]
    ids = [jnp.where(valid, row * NX * BLOCKS + lane, -1) for row in range(NTM // NX)]
    found = [jnp.zeros((BLOCKS, BLK), jnp.float32) for _ in ids]
    for j in range(KFAR):
        column = jnp.broadcast_to(mine[:, j : j + 1], (BLOCKS, BLK))
        found = [jnp.where(column == i, 1.0, f) for i, f in zip(ids, found)]
    present += [jnp.max(f, axis=0, keepdims=True) for f in found]
    present = jnp.concatenate(present, axis=0)

    a = lax.broadcasted_iota(jnp.int32, (BLK, BLK), 0)
    b = lax.broadcasted_iota(jnp.int32, (BLK, BLK), 1)
    group_a, group_b = (a * 2731) >> 16, (b * 2731) >> 16
    before = jnp.where((group_a == group_b) & (a < b), 1.0, 0.0).astype(jnp.bfloat16)
    rank = jnp.dot(present.astype(jnp.bfloat16), before, preferred_element_type=jnp.float32)

    receivers = NZ * NC
    chosen = [
        jnp.where((present[:receivers] > 0) & (rank[:receivers] == k), within.astype(jnp.float32), 0.0)
        for k in range(CAP)
    ]
    gather = jnp.where(group_a == b, 1.0, 0.0).astype(jnp.bfloat16)
    picks = jnp.dot(
        jnp.concatenate(chosen, axis=0).astype(jnp.bfloat16),
        gather,
        preferred_element_type=jnp.float32,
    )
    picks_ref[...] = picks.astype(jnp.int32)

    lies = []
    for row in range(NTM // NX):
        device = row * NX + group
        dz = (z - (device >> 3)) & 3
        dx = (x - (device >> 1)) & 3
        dc = core ^ (device & 1)
        start = ((dc * NZ + dz) * NX + dx) * CAP
        lies.append(start.astype(jnp.float32) + rank[receivers + row : receivers + row + 1])
    entry = lax.broadcasted_iota(jnp.int32, (BLOCKS, KFAR), 1)
    slots = jnp.zeros((BLOCKS, KFAR), jnp.float32)
    for j in range(KFAR):
        column = jnp.broadcast_to(mine[:, j : j + 1], (BLOCKS, BLK))
        at = jnp.zeros((BLOCKS, BLK), jnp.float32)
        for i, where in zip(ids, lies):
            at = jnp.where(column == i, where, at)
        slots = jnp.where(entry == j, jnp.sum(at, axis=1, keepdims=True), slots)

    row = lax.broadcasted_iota(jnp.int32, (BLOCKS, KFAR), 0)
    frame = t * (BLOCKS // FRAME_BLK) + jnp.where(row >= FRAME_BLK, 1, 0)
    distance = jnp.abs(frame - ((mine * 5462) >> 16))
    strides = jnp.zeros((BLOCKS, KFAR), jnp.int32)
    for d in range(steps.shape[0]):
        strides = jnp.where(distance == d, steps[d], strides)

    local = near_ref[...] - t * BLOCKS
    local = jnp.where(local < 0, local + FRAME_BLK + BLOCKS, local)
    rest = jnp.zeros((BLOCKS, BLK - KNEAR - 2 * KFAR), jnp.int32)
    table_ref[:BLOCKS, :] = jnp.concatenate(
        [local, slots.astype(jnp.int32), strides, rest], axis=1
    )

    h = scalars[1]
    order = jnp.zeros((8, BLK), jnp.int32)
    column = lax.broadcasted_iota(jnp.int32, (8, BLK), 1)
    for at, half in ((FAST_FIRST, 1 - core), (SLOW_FIRST, core)):
        inside = (h >> 1) == half
        order = jnp.where(column == at, jnp.where(inside, h ^ 1, h ^ 2), order)
        order = jnp.where(column == at + 1, jnp.where(inside, h, h ^ 3), order)
    table_ref[BLOCKS:, :] = order


def index_work(scalars, steps, far_list, near_list):
    whole = lambda shape: pl.BlockSpec(shape, lambda i, *_: (0, 0))
    shapes = [(NZ * NC * CAP, BLK), (BLOCKS + 8, BLK)]
    return pl.pallas_call(
        index_kernel,
        grid_spec=pltpu.PrefetchScalarGridSpec(
            num_scalar_prefetch=2,
            grid=(1,),
            in_specs=[whole(far_list.shape), whole(near_list.shape)],
            out_specs=[whole(shape) for shape in shapes],
        ),
        out_shape=[jax.ShapeDtypeStruct(shape, jnp.int32) for shape in shapes],
        cost_estimate=pl.CostEstimate(flops=2**20, bytes_accessed=2**22, transcendentals=0),
    )(scalars, steps, far_list, near_list)


def pack_kernel(scalars, k_fast, v_fast, k_slow, v_slow, thin_ref, fast_ref, slow_ref):
    core, step = scalars[0] & 1, pl.program_id(0)
    blocks = k_fast.shape[0] // BLK

    def thin(ref):
        rows = ref[...].astype(jnp.float32).reshape(blocks * THIN, MINSTRIDE, WIDTH)
        return rows[:, 0, :]

    for out, frame, k_part, v_part in (
        (fast_ref, 1 - core, k_fast, v_fast),
        (slow_ref, core, k_slow, v_slow),
    ):
        out[0] = k_part[...]
        out[1] = v_part[...]
        keys, values = thin(k_part), thin(v_part)
        pairs = [a[b * THIN : b * THIN + THIN] for b in range(blocks) for a in (keys, values)]
        first = (frame * FRAME_BLK + step * blocks) * 2 * THIN
        rows = pl.ds(pl.multiple_of(first, 2 * THIN), blocks * 2 * THIN)
        thin_ref[rows, :] = jnp.concatenate(pairs, axis=0).astype(jnp.bfloat16)


def pack(scalars, keys, values):
    parts = 4
    rows = FRAME // parts
    fast = pl.BlockSpec((rows, WIDTH), lambda i, s: ((1 - (s[0] & 1)) * parts + i, 0))
    slow = pl.BlockSpec((rows, WIDTH), lambda i, s: ((s[0] & 1) * parts + i, 0))
    frame = jax.ShapeDtypeStruct((2, FRAME, WIDTH), jnp.bfloat16)
    thinned = jax.ShapeDtypeStruct((BLOCKS * 2 * THIN, WIDTH), jnp.bfloat16)
    thinned, *frames = pl.pallas_call(
        pack_kernel,
        grid_spec=pltpu.PrefetchScalarGridSpec(
            num_scalar_prefetch=1,
            grid=(parts,),
            in_specs=[fast, fast, slow, slow],
            out_specs=[pl.BlockSpec(thinned.shape, lambda i, s: (0, 0))]
            + [pl.BlockSpec((2, rows, WIDTH), lambda i, s: (0, i, 0))] * 2,
        ),
        out_shape=[thinned, frame, frame],
        cost_estimate=pl.CostEstimate(flops=0, bytes_accessed=10 * 2**20, transcendentals=0),
    )(scalars, keys, values, keys, values)
    return thinned, *(f.reshape(2 * FRAME, WIDTH) for f in frames)


def pass_kernel(a, b, c, d, after, out_ref):
    rows = a.shape[0]
    for n, ref in enumerate((a, b, c, d)):
        out_ref[n * rows : n * rows + rows, :] = ref[...]


def pack_passed(arrived, after):
    rows = arrived[0].shape[0] // 2
    return pl.pallas_call(
        pass_kernel,
        grid=(1,),
        in_specs=[pl.BlockSpec((rows, WIDTH), lambda i: (1, 0))] * NZ + [ANYWHERE],
        out_specs=pl.BlockSpec((NZ * rows, WIDTH), lambda i: (0, 0)),
        out_shape=jax.ShapeDtypeStruct((NZ * rows, WIDTH), jnp.bfloat16),
        cost_estimate=pl.CostEstimate(flops=0, bytes_accessed=2 * 2**20, transcendentals=0),
    )(*arrived, after)


def select_kernel(picks, *refs):
    sources, outs = refs[:NX], refs[NX + 1 :]
    for dz, out in enumerate(outs):
        for dc in range(NC):
            for s in range(NX):
                for k in range(CAP):
                    block = picks[k * NZ * NC + dz * NC + dc, s]
                    at = pl.ds(pl.multiple_of(block * 2 * THIN, 2 * THIN), 2 * THIN)
                    to = ((dc * NX + s) * CAP + k) * 2 * THIN
                    out[to : to + 2 * THIN, :] = sources[s][at, :]


def select(picks, sources, after):
    shape = jax.ShapeDtypeStruct((NC * NX * CAP * 2 * THIN, WIDTH), jnp.bfloat16)
    whole = lambda a: pl.BlockSpec(a.shape, lambda i, *_: (0, 0))
    return pl.pallas_call(
        select_kernel,
        grid_spec=pltpu.PrefetchScalarGridSpec(
            num_scalar_prefetch=1,
            grid=(1,),
            in_specs=[whole(s) for s in sources] + [ANYWHERE],
            out_specs=[whole(shape)] * NZ,
        ),
        out_shape=[shape] * NZ,
        compiler_params=pltpu.CompilerParams(vmem_limit_bytes=VMEM_LIMIT),
        cost_estimate=pl.CostEstimate(flops=0, bytes_accessed=4 * 2**20, transcendentals=0),
    )(picks, *sources, after)


ROW_TILE = 256


def project_kernel(scalars, *refs, wanted_fast, held):
    parts, (weight, w_one, w_two, w_swap) = refs[:4], refs[4:8]
    out_ref, out_vm, sems = refs[8 + held :]
    core, h = scalars[0] & 1, scalars[1]
    gets_fast = (h >> 1) == 1 - core
    tiles = out_vm.shape[0] // ROW_TILE
    width = out_vm.shape[1] // NC

    def copy_of(i):
        rows = pl.ds(pl.multiple_of(i * ROW_TILE, ROW_TILE), ROW_TILE)
        return pltpu.make_async_copy(out_vm.at[rows], out_ref.at[rows], sems.at[i])

    def group(n):
        return pl.ds(n * WIDTH, WIDTH)

    for mine in range(NC):

        @pl.when((core == mine) & (gets_fast == wanted_fast))
        def _(mine=mine):
            def step(i, _):
                rows = pl.ds(pl.multiple_of(i * ROW_TILE, ROW_TILE), ROW_TILE)
                attended = jnp.concatenate([part[rows, :] for part in parts], axis=1)
                for half in range(NC):
                    cols = pl.ds(half * width, width)
                    if half == mine:
                        others = w_one[...], w_two[group(1), :], w_two[group(0), :]
                    else:
                        others = w_swap[group(0), :], w_swap[group(2), :], w_swap[group(1), :]
                    out_vm[rows, cols] = jnp.dot(
                        attended,
                        jnp.concatenate([weight[:, cols], *others], axis=0),
                        preferred_element_type=jnp.float32,
                    ).astype(jnp.bfloat16)
                copy_of(i).start()
                return 0

            lax.fori_loop(0, tiles, step, 0)
            for i in range(tiles):
                copy_of(i).wait()


def project(scalars, parts, weights, wanted_fast, held=None):
    rows, width = CHUNK * BLK, weights[0].shape[1]
    inputs = (*parts, *weights)
    extra = () if held is None else (held,)
    return pl.pallas_call(
        functools.partial(project_kernel, wanted_fast=wanted_fast, held=len(extra)),
        grid_spec=pltpu.PrefetchScalarGridSpec(
            num_scalar_prefetch=1,
            grid=(1,),
            in_specs=[IN_VMEM] * len(inputs) + [IN_HBM] * len(extra),
            out_specs=IN_HBM,
            scratch_shapes=[
                pltpu.VMEM((rows, width), jnp.bfloat16),
                pltpu.SemaphoreType.DMA((rows // ROW_TILE,)),
            ],
        ),
        out_shape=jax.ShapeDtypeStruct((rows, width), jnp.bfloat16),
        input_output_aliases={} if held is None else {1 + len(inputs): 0},
        compiler_params=pltpu.CompilerParams(vmem_limit_bytes=24 * 2**20),
        cost_estimate=pl.CostEstimate(
            flops=2 * rows * NHEAD * WIDTH * width, bytes_accessed=10 * 2**20, transcendentals=0
        ),
    )(scalars, *inputs, *extra)


def per_device(query, keys, values, out_weight, near_list, far_list, stride_table):
    t = lax.axis_index("tm")
    h = lax.axis_index("head")
    coords = [(zz, xx, cc) for zz in range(NZ) for xx in range(NX) for cc in range(NC)]
    swap = [(i, i ^ 1) for i in range(NTM)]
    across = [(i, i + 1) for i in range(1, NTM - 1, 2)]
    across = across + [(j, i) for i, j in across]
    place = jnp.stack([t, h]).astype(jnp.int32)

    thinned, fast_part, slow_part = pack(place, keys, values)
    along_x = [
        lax.ppermute(
            thinned, "tm", [(tm_index(*p), tm_index(p[0], p[1] + d, p[2])) for p in coords]
        )
        for d in range(1, NX)
    ]

    halo_fast = lax.ppermute(fast_part, "tm", swap)
    picks, table = index_work(place, stride_table, far_list, near_list)
    slow_part, table, *along_x = lax.optimization_barrier((slow_part, table, *along_x))
    halo_slow = lax.ppermute(slow_part, "tm", across)

    near_fast = attend(table, query, keys, values, halo_fast, None, FAST_FIRST, 2)
    packs = select(picks, [thinned] + along_x, near_fast[1])
    arrived = [packs[0]]
    for d in range(1, NZ):
        pairs = [(tm_index(*p), tm_index(p[0] + d, p[1], p[2])) for p in coords]
        arrived.append(lax.ppermute(packs[d], "tm", pairs))

    cols = out_weight.shape[1] // NC
    half = lax.dynamic_slice_in_dim(out_weight, (t % NC) * cols, cols, 1)
    half, _ = lax.optimization_barrier((half, table))
    w_one = lax.ppermute(half, "head", [(g, g ^ 1) for g in range(NHEAD)])
    half, w_one, _ = lax.optimization_barrier((half, w_one, packs[0]))
    w_two = lax.ppermute(
        jnp.concatenate([half, w_one], axis=0), "head", [(g, g ^ 3) for g in range(NHEAD)]
    )

    near_slow = attend(
        table, query, keys, values, halo_slow, None, SLOW_FIRST, 2, (packs[0],)
    )
    passed = lax.ppermute(pack_passed(arrived, near_slow[1]), "tm", swap)
    far = [*arrived, passed]
    w_swap = lax.ppermute(jnp.concatenate([w_one, w_two], axis=0), "tm", swap)
    first_fast, last_fast = merge_far(table, query, near_fast, far, FAST_FIRST, near_slow[1])
    near_slow, first_fast = lax.optimization_barrier((near_slow, first_fast))
    first_slow, last_slow = merge_far(table, query, near_slow, far, SLOW_FIRST, w_swap)

    def exchange(chunk, e, fast):
        pairs = []
        for i in range(NTM):
            frame = (1 - i % NC) if fast else i % NC
            for g in range(NHEAD):
                if (e >= 2) == (g // 2 != frame):
                    pairs.append((i * NHEAD + g, i * NHEAD + (g ^ e)))
        return lax.ppermute(chunk, ("tm", "head"), pairs)

    def received(first, last, fast):
        one, two, three = [
            exchange(chunk, e, fast) for e, chunk in ((1, first), (2, first), (3, last))
        ]
        return last, one, two, three

    weights = (out_weight, w_one, w_two, w_swap)
    fast = received(first_fast, last_fast, True)
    slow = received(first_slow, last_slow, False)
    held = project(place, fast, weights, True)
    return project(place, slow, weights, False, held)


def solution(mesh):
    placed = (
        P("tm", "head"),
        P("tm", "head"),
        P("tm", "head"),
        P("head", None),
        P("tm", None),
        P(),
        P(),
    )
    return jax.shard_map(
        per_device, mesh=mesh, in_specs=placed, out_specs=P(("tm", "head"), None), check_vma=False
    )
```

```python
import functools
import math

import jax
import jax.numpy as jnp
from jax import lax
from jax.experimental import pallas as pl
from jax.experimental.pallas import tpu as pltpu
from jax.sharding import PartitionSpec as P

HD = 128
BLK = 128
FRAME_BLK = 12
KNEAR = 16
KFAR = 16
CAP = 6
MINSTRIDE = 16
THIN = BLK // MINSTRIDE
HEADS = 3
WIDTH = HEADS * HD
BLOCKS = 24
NX, NZ, NC = 4, 4, 2
NTM = NX * NZ * NC
NHEAD = 4
CHUNK = BLOCKS // NHEAD
FAR_ROWS = NTM * CAP * 2 * THIN
FRAME = FRAME_BLK * BLK
LOG2_SCALE = math.log2(math.e) / math.sqrt(HD)
NT = (((1,), (1,)), ((), ()))
VMEM_LIMIT = 56 * 2**20
UNROLL = 6
SLOT, STRIDE, ORDER = KNEAR, KNEAR + KFAR, BLOCKS
FAST_FIRST, FAST_LAST, SLOW_FIRST, SLOW_LAST = range(4)
IN_HBM = pl.BlockSpec(memory_space=pltpu.HBM)
ANYWHERE = pl.BlockSpec(memory_space=pl.ANY)
IN_VMEM = pl.BlockSpec(memory_space=pltpu.VMEM)


def tm_index(z, x, c):
    return (z % NZ) * NX * NC + (x % NX) * NC + c


def load_far(far_refs, far_vm, sems, first_sem):
    part = NX * CAP * 2 * THIN
    copies = []
    for n, ref in enumerate(far_refs):
        rows = part if n < NZ else NZ * part
        copies.append(
            pltpu.make_async_copy(
                ref.at[pl.ds(0, rows)], far_vm.at[pl.ds(n * part, rows)], sems.at[first_sem + n]
            )
        )
    return copies


def far_block(far_vm, table, block):
    tiles = [
        far_vm[
            pl.ds(pl.multiple_of(table[block, SLOT + j] * 2 * THIN, 2 * THIN), 2 * THIN), :
        ].astype(jnp.float32)
        for j in range(KFAR)
    ]
    keys = jnp.concatenate([t[:THIN] for t in tiles], axis=0).astype(jnp.bfloat16)
    values = jnp.concatenate([t[THIN:] for t in tiles], axis=0).astype(jnp.bfloat16)
    lane = lax.broadcasted_iota(jnp.int32, (1, BLK), 1)
    stride = jnp.zeros((1, BLK), jnp.int32)
    for j in range(KFAR):
        stride = jnp.where(lane // THIN == j, table[block, STRIDE + j], stride)
    used = (((lane % THIN) * MINSTRIDE) & (stride - 1)) == 0
    return keys, values, used


def with_ones(values):
    return jnp.concatenate([values, jnp.ones((values.shape[0], HD), jnp.bfloat16)], axis=1)


def attend_kernel(table, q_ref, k_ref, v_ref, halo_ref, *rest, chunk, with_far, ordering):
    rest = rest[ordering:]
    if with_far:
        far_refs, (out_ref, k_vm, v_vm, s_vm, far_vm, sems) = rest[:5], rest[5:]
    else:
        near_ref, level_ref, k_vm, v_vm, s_vm, sems = rest
    step = pl.program_id(0)
    own = BLOCKS * BLK
    halo = pl.ds(own, FRAME)
    key_copies = [
        pltpu.make_async_copy(k_ref, k_vm.at[pl.ds(0, own)], sems.at[0]),
        pltpu.make_async_copy(halo_ref.at[pl.ds(0, FRAME)], k_vm.at[halo], sems.at[1]),
    ]
    value_copies = [
        pltpu.make_async_copy(v_ref, v_vm.at[pl.ds(0, own)], sems.at[2]),
        pltpu.make_async_copy(halo_ref.at[pl.ds(FRAME, FRAME)], v_vm.at[halo], sems.at[3]),
    ]
    if with_far:
        key_copies += load_far(far_refs, far_vm, sems, 4)

    @pl.when(step == 0)
    def _():
        for copy in key_copies + value_copies:
            copy.start()
        for copy in key_copies:
            copy.wait()

    first = table[ORDER, chunk + step] * CHUNK

    def prepare(unit):
        block = first + unit
        offsets = [pl.multiple_of(table[block, j] * BLK, BLK) for j in range(KNEAR)]
        far = far_block(far_vm, table, block) if with_far else None
        return offsets, far, pl.ds(pl.multiple_of(unit * BLK, BLK), BLK)

    count = KNEAR + (1 if with_far else 0)

    def score_pair(prepared, head, j):
        offsets, far, rows = prepared
        cols = slice(head * HD, head * HD + HD)
        query = q_ref[rows, cols]
        if j < KNEAR:
            keys = jnp.concatenate([k_vm[pl.ds(o, BLK), cols] for o in offsets[j : j + 2]], axis=0)
            both = lax.dot_general(query, keys, NT, preferred_element_type=jnp.float32)
            return [both[:, :BLK], both[:, BLK:]]
        last = lax.dot_general(query, far[0][:, cols], NT, preferred_element_type=jnp.float32)
        return [jnp.where(far[2], last, -1e30)]

    def peak_of(scores):
        top = functools.reduce(jnp.maximum, scores)
        return jnp.max(top, axis=1, keepdims=True) * LOG2_SCALE

    def add_pair(acc, prepared, head, scores, peak, j):
        offsets, far, _ = prepared
        cols = slice(head * HD, head * HD + HD)
        some = range(j, min(j + 2, count))
        weights = jnp.concatenate(
            [jnp.exp2(scores[i] * LOG2_SCALE - peak).astype(jnp.bfloat16) for i in some], axis=1
        )
        values = jnp.concatenate(
            [v_vm[pl.ds(offsets[i], BLK), cols] if i < KNEAR else far[1][:, cols] for i in some],
            axis=0,
        )
        part = jnp.dot(weights, with_ones(values), preferred_element_type=jnp.float32)
        return part if acc is None else acc + part

    def store(prepared, head, peak, acc):
        rows = prepared[2]
        cols = slice(head * HD, head * HD + HD)
        if with_far:
            out_ref[rows, cols] = (acc[:, :HD] / acc[:, HD:]).astype(jnp.bfloat16)
        else:
            near_ref[rows, cols] = (acc[:, :HD] / acc[:, HD:]).astype(jnp.bfloat16)
            level_ref[rows, cols] = peak + jnp.log2(acc[:, HD:])

    def scores_of(prepared, head):
        scores = []
        for j in range(0, count, 2):
            scores += score_pair(prepared, head, j)
        return scores

    def overlap(fresh, pending):
        prepared, head, scores = pending
        peak = peak_of(scores)
        following, acc = [], None
        for j in range(0, count, 2):
            following += score_pair(*fresh, j)
            acc = add_pair(acc, prepared, head, scores, peak, j)
        store(prepared, head, peak, acc)
        return following

    def hold(scores):
        for i, some in enumerate(scores):
            s_vm[:, i * BLK : i * BLK + BLK] = some

    hold(scores_of(prepare(0), 0))

    @pl.when(step == 0)
    def _():
        for copy in value_copies:
            copy.wait()

    units = CHUNK // UNROLL

    def body(i, _):
        pending = None
        scores = [s_vm[:, n * BLK : n * BLK + BLK] for n in range(count)]
        for u in range(UNROLL):
            unit = i * UNROLL + u
            prepared = prepare(unit)
            for head in range(HEADS):
                if head or u:
                    scores = overlap((prepared, head), pending)
                pending = prepared, head, scores
        after = prepare(jnp.minimum(i * UNROLL + UNROLL, CHUNK - 1))
        hold(overlap((after, 0), pending))
        return 0

    lax.fori_loop(0, units, body, 0)


def attend(table, query, keys, values, halo, far, chunk, chunks, after=()):
    with_far = far is not None
    spot = lambda i, s: (s[ORDER, chunk + i], 0)
    same = lambda i, s: (i, 0)
    rows = CHUNK * BLK
    scratch = [pltpu.VMEM((BLOCKS * BLK + FRAME, WIDTH), jnp.bfloat16) for _ in range(2)]
    scratch.append(pltpu.VMEM((BLK, (KNEAR + 1) * BLK), jnp.float32))
    if with_far:
        scratch.append(pltpu.VMEM((FAR_ROWS, WIDTH), jnp.bfloat16))
        out_shape = jax.ShapeDtypeStruct((chunks * rows, WIDTH), jnp.bfloat16)
        out_specs = pl.BlockSpec((rows, WIDTH), same)
    else:
        out_shape = [
            jax.ShapeDtypeStruct((chunks * rows, WIDTH), kind)
            for kind in (jnp.bfloat16, jnp.float32)
        ]
        out_specs = [pl.BlockSpec((rows, WIDTH), same)] * 2
    scratch.append(pltpu.SemaphoreType.DMA((9,)))
    extra = tuple(far) if with_far else ()
    return pl.pallas_call(
        functools.partial(
            attend_kernel, chunk=chunk, with_far=with_far, ordering=len(after)
        ),
        grid_spec=pltpu.PrefetchScalarGridSpec(
            num_scalar_prefetch=1,
            grid=(chunks,),
            in_specs=[pl.BlockSpec((rows, WIDTH), spot)] + [IN_HBM] * 3 + [ANYWHERE] * len(after + extra),
            out_specs=out_specs,
            scratch_shapes=scratch,
        ),
        out_shape=out_shape,
        compiler_params=pltpu.CompilerParams(vmem_limit_bytes=VMEM_LIMIT),
        cost_estimate=pl.CostEstimate(
            flops=chunks * CHUNK * HEADS * 17 * 4 * BLK * BLK * HD * 3,
            bytes_accessed=8 * 2**20,
            transcendentals=0,
        ),
    )(table, query, keys, values, halo, *after, *extra)


def merge_kernel(table, q_ref, near_ref, level_ref, *rest, chunk):
    far_refs, (_, first_ref, last_ref, out_vm, far_vm, sems) = rest[:5], rest[5:]
    step = pl.program_id(0)

    @pl.when(step == 0)
    def _():
        copies = load_far(far_refs, far_vm, sems, 0)
        for copy in copies:
            copy.start()
        for copy in copies:
            copy.wait()

    first = table[ORDER, chunk + step] * CHUNK
    spot = {
        (unit, head): (
            slice(unit * BLK, unit * BLK + BLK),
            slice(head * HD, head * HD + HD),
        )
        for unit in range(CHUNK)
        for head in range(HEADS)
    }
    far = [far_block(far_vm, table, first + unit) for unit in range(CHUNK)]
    scores, peaks, sums = {}, {}, {}
    for p, (rows, cols) in spot.items():
        keys, _, used = far[p[0]]
        some = lax.dot_general(
            q_ref[rows, cols], keys[:, cols], NT, preferred_element_type=jnp.float32
        )
        scores[p] = jnp.where(used, some, -1e30) * LOG2_SCALE
    for p, (rows, cols) in spot.items():
        peaks[p] = jnp.maximum(jnp.max(scores[p], axis=1, keepdims=True), level_ref[rows, cols])
    for p, (rows, cols) in spot.items():
        weights = jnp.exp2(scores[p] - peaks[p]).astype(jnp.bfloat16)
        values = far[p[0]][1][:, cols]
        sums[p] = jnp.dot(weights, with_ones(values), preferred_element_type=jnp.float32)
    for p, (rows, cols) in spot.items():
        share = jnp.exp2(level_ref[rows, cols] - peaks[p])
        total = share + sums[p][:, HD:]
        mixed = near_ref[rows, cols].astype(jnp.float32) * share + sums[p][:, :HD]
        out_vm[step, rows, cols] = (mixed / total).astype(jnp.bfloat16)

    outs = [
        pltpu.make_async_copy(out_vm.at[n], ref, sems.at[5 + n])
        for n, ref in enumerate((first_ref, last_ref))
    ]

    @pl.when(step == 0)
    def _():
        outs[0].start()

    @pl.when(step == 1)
    def _():
        outs[1].start()
        for copy in outs:
            copy.wait()


def merge_far(table, query, state, far, chunk, after):
    rows = CHUNK * BLK
    return pl.pallas_call(
        functools.partial(merge_kernel, chunk=chunk),
        grid_spec=pltpu.PrefetchScalarGridSpec(
            num_scalar_prefetch=1,
            grid=(2,),
            in_specs=[pl.BlockSpec((rows, WIDTH), lambda i, s: (s[ORDER, chunk + i], 0))]
            + [pl.BlockSpec((rows, WIDTH), lambda i, s: (i, 0))] * 2
            + [ANYWHERE] * 6,
            out_specs=[IN_HBM] * 2,
            scratch_shapes=[
                pltpu.VMEM((2, rows, WIDTH), jnp.bfloat16),
                pltpu.VMEM((FAR_ROWS, WIDTH), jnp.bfloat16),
                pltpu.SemaphoreType.DMA((7,)),
            ],
        ),
        out_shape=[jax.ShapeDtypeStruct((rows, WIDTH), jnp.bfloat16)] * 2,
        compiler_params=pltpu.CompilerParams(vmem_limit_bytes=VMEM_LIMIT),
        cost_estimate=pl.CostEstimate(
            flops=2 * CHUNK * HEADS * 4 * BLK * BLK * HD * 6,
            bytes_accessed=8 * 2**20,
            transcendentals=0,
        ),
    )(table, query, *state, *far, after)


def index_kernel(scalars, steps, far_ref, near_ref, picks_ref, table_ref):
    t = scalars[0]
    core, x, z = t & 1, (t >> 1) & 3, t >> 3
    lane = lax.broadcasted_iota(jnp.int32, (1, BLK), 1)
    group = (lane * 2731) >> 16
    within = lane - group * BLOCKS
    valid = lane < NX * BLOCKS

    source = ((z * NX + ((x - group) & 3)) * NC + core) * BLOCKS + within
    source = jnp.where(valid, source, -1)
    present = []
    for dz in range(NZ):
        for dc in range(NC):
            receiver = (((z + dz) & 3) * NX + x) * NC + (core ^ dc)
            listed = far_ref[pl.ds(pl.multiple_of(receiver * BLOCKS, 8), BLOCKS), :]
            found = jnp.zeros((BLOCKS, BLK), jnp.float32)
            for j in range(KFAR):
                found = jnp.where(listed[:, j : j + 1] == source, 1.0, found)
            present.append(jnp.max(found, axis=0, keepdims=True))

    mine = far_ref[pl.ds(pl.multiple_of(t * BLOCKS, 8), BLOCKS), :]
    ids = [jnp.where(valid, row * NX * BLOCKS + lane, -1) for row in range(NTM // NX)]
    found = [jnp.zeros((BLOCKS, BLK), jnp.float32) for _ in ids]
    for j in range(KFAR):
        column = jnp.broadcast_to(mine[:, j : j + 1], (BLOCKS, BLK))
        found = [jnp.where(column == i, 1.0, f) for i, f in zip(ids, found)]
    present += [jnp.max(f, axis=0, keepdims=True) for f in found]
    present = jnp.concatenate(present, axis=0)

    a = lax.broadcasted_iota(jnp.int32, (BLK, BLK), 0)
    b = lax.broadcasted_iota(jnp.int32, (BLK, BLK), 1)
    group_a, group_b = (a * 2731) >> 16, (b * 2731) >> 16
    before = jnp.where((group_a == group_b) & (a < b), 1.0, 0.0).astype(jnp.bfloat16)
    rank = jnp.dot(present.astype(jnp.bfloat16), before, preferred_element_type=jnp.float32)

    receivers = NZ * NC
    chosen = [
        jnp.where((present[:receivers] > 0) & (rank[:receivers] == k), within.astype(jnp.float32), 0.0)
        for k in range(CAP)
    ]
    gather = jnp.where(group_a == b, 1.0, 0.0).astype(jnp.bfloat16)
    picks = jnp.dot(
        jnp.concatenate(chosen, axis=0).astype(jnp.bfloat16),
        gather,
        preferred_element_type=jnp.float32,
    )
    picks_ref[...] = picks.astype(jnp.int32)

    lies = []
    for row in range(NTM // NX):
        device = row * NX + group
        dz = (z - (device >> 3)) & 3
        dx = (x - (device >> 1)) & 3
        dc = core ^ (device & 1)
        start = ((dc * NZ + dz) * NX + dx) * CAP
        lies.append(start.astype(jnp.float32) + rank[receivers + row : receivers + row + 1])
    entry = lax.broadcasted_iota(jnp.int32, (BLOCKS, KFAR), 1)
    slots = jnp.zeros((BLOCKS, KFAR), jnp.float32)
    for j in range(KFAR):
        column = jnp.broadcast_to(mine[:, j : j + 1], (BLOCKS, BLK))
        at = jnp.zeros((BLOCKS, BLK), jnp.float32)
        for i, where in zip(ids, lies):
            at = jnp.where(column == i, where, at)
        slots = jnp.where(entry == j, jnp.sum(at, axis=1, keepdims=True), slots)

    row = lax.broadcasted_iota(jnp.int32, (BLOCKS, KFAR), 0)
    frame = t * (BLOCKS // FRAME_BLK) + jnp.where(row >= FRAME_BLK, 1, 0)
    distance = jnp.abs(frame - ((mine * 5462) >> 16))
    strides = jnp.zeros((BLOCKS, KFAR), jnp.int32)
    for d in range(steps.shape[0]):
        strides = jnp.where(distance == d, steps[d], strides)

    local = near_ref[...] - t * BLOCKS
    local = jnp.where(local < 0, local + FRAME_BLK + BLOCKS, local)
    rest = jnp.zeros((BLOCKS, BLK - KNEAR - 2 * KFAR), jnp.int32)
    table_ref[:BLOCKS, :] = jnp.concatenate(
        [local, slots.astype(jnp.int32), strides, rest], axis=1
    )

    h = scalars[1]
    order = jnp.zeros((8, BLK), jnp.int32)
    column = lax.broadcasted_iota(jnp.int32, (8, BLK), 1)
    for at, half in ((FAST_FIRST, 1 - core), (SLOW_FIRST, core)):
        inside = (h >> 1) == half
        order = jnp.where(column == at, jnp.where(inside, h ^ 1, h ^ 2), order)
        order = jnp.where(column == at + 1, jnp.where(inside, h, h ^ 3), order)
    table_ref[BLOCKS:, :] = order


def index_work(scalars, steps, far_list, near_list):
    whole = lambda shape: pl.BlockSpec(shape, lambda i, *_: (0, 0))
    shapes = [(NZ * NC * CAP, BLK), (BLOCKS + 8, BLK)]
    return pl.pallas_call(
        index_kernel,
        grid_spec=pltpu.PrefetchScalarGridSpec(
            num_scalar_prefetch=2,
            grid=(1,),
            in_specs=[whole(far_list.shape), whole(near_list.shape)],
            out_specs=[whole(shape) for shape in shapes],
        ),
        out_shape=[jax.ShapeDtypeStruct(shape, jnp.int32) for shape in shapes],
        cost_estimate=pl.CostEstimate(flops=2**20, bytes_accessed=2**22, transcendentals=0),
    )(scalars, steps, far_list, near_list)


def pack_kernel(scalars, k_fast, v_fast, k_slow, v_slow, thin_ref, fast_ref, slow_ref):
    core, step = scalars[0] & 1, pl.program_id(0)
    blocks = k_fast.shape[0] // BLK

    def thin(ref):
        rows = ref[...].astype(jnp.float32).reshape(blocks * THIN, MINSTRIDE, WIDTH)
        return rows[:, 0, :]

    for out, frame, k_part, v_part in (
        (fast_ref, 1 - core, k_fast, v_fast),
        (slow_ref, core, k_slow, v_slow),
    ):
        out[0] = k_part[...]
        out[1] = v_part[...]
        keys, values = thin(k_part), thin(v_part)
        pairs = [a[b * THIN : b * THIN + THIN] for b in range(blocks) for a in (keys, values)]
        first = (frame * FRAME_BLK + step * blocks) * 2 * THIN
        rows = pl.ds(pl.multiple_of(first, 2 * THIN), blocks * 2 * THIN)
        thin_ref[rows, :] = jnp.concatenate(pairs, axis=0).astype(jnp.bfloat16)


def pack(scalars, keys, values):
    parts = 4
    rows = FRAME // parts
    fast = pl.BlockSpec((rows, WIDTH), lambda i, s: ((1 - (s[0] & 1)) * parts + i, 0))
    slow = pl.BlockSpec((rows, WIDTH), lambda i, s: ((s[0] & 1) * parts + i, 0))
    frame = jax.ShapeDtypeStruct((2, FRAME, WIDTH), jnp.bfloat16)
    thinned = jax.ShapeDtypeStruct((BLOCKS * 2 * THIN, WIDTH), jnp.bfloat16)
    thinned, *frames = pl.pallas_call(
        pack_kernel,
        grid_spec=pltpu.PrefetchScalarGridSpec(
            num_scalar_prefetch=1,
            grid=(parts,),
            in_specs=[fast, fast, slow, slow],
            out_specs=[pl.BlockSpec(thinned.shape, lambda i, s: (0, 0))]
            + [pl.BlockSpec((2, rows, WIDTH), lambda i, s: (0, i, 0))] * 2,
        ),
        out_shape=[thinned, frame, frame],
        cost_estimate=pl.CostEstimate(flops=0, bytes_accessed=10 * 2**20, transcendentals=0),
    )(scalars, keys, values, keys, values)
    return thinned, *(f.reshape(2 * FRAME, WIDTH) for f in frames)


def pass_kernel(a, b, c, d, after, out_ref):
    rows = a.shape[0]
    for n, ref in enumerate((a, b, c, d)):
        out_ref[n * rows : n * rows + rows, :] = ref[...]


def pack_passed(arrived, after):
    rows = arrived[0].shape[0] // 2
    return pl.pallas_call(
        pass_kernel,
        grid=(1,),
        in_specs=[pl.BlockSpec((rows, WIDTH), lambda i: (1, 0))] * NZ + [ANYWHERE],
        out_specs=pl.BlockSpec((NZ * rows, WIDTH), lambda i: (0, 0)),
        out_shape=jax.ShapeDtypeStruct((NZ * rows, WIDTH), jnp.bfloat16),
        cost_estimate=pl.CostEstimate(flops=0, bytes_accessed=2 * 2**20, transcendentals=0),
    )(*arrived, after)


def select_kernel(picks, *refs):
    sources, outs = refs[:NX], refs[NX + 1 :]
    for dz, out in enumerate(outs):
        for dc in range(NC):
            for s in range(NX):
                for k in range(CAP):
                    block = picks[k * NZ * NC + dz * NC + dc, s]
                    at = pl.ds(pl.multiple_of(block * 2 * THIN, 2 * THIN), 2 * THIN)
                    to = ((dc * NX + s) * CAP + k) * 2 * THIN
                    out[to : to + 2 * THIN, :] = sources[s][at, :]


def select(picks, sources, after):
    shape = jax.ShapeDtypeStruct((NC * NX * CAP * 2 * THIN, WIDTH), jnp.bfloat16)
    whole = lambda a: pl.BlockSpec(a.shape, lambda i, *_: (0, 0))
    return pl.pallas_call(
        select_kernel,
        grid_spec=pltpu.PrefetchScalarGridSpec(
            num_scalar_prefetch=1,
            grid=(1,),
            in_specs=[whole(s) for s in sources] + [ANYWHERE],
            out_specs=[whole(shape)] * NZ,
        ),
        out_shape=[shape] * NZ,
        compiler_params=pltpu.CompilerParams(vmem_limit_bytes=VMEM_LIMIT),
        cost_estimate=pl.CostEstimate(flops=0, bytes_accessed=4 * 2**20, transcendentals=0),
    )(picks, *sources, after)


ROW_TILE = 256


def project_kernel(scalars, *refs, wanted_fast, held):
    parts, (weight, w_one, w_two, w_swap) = refs[:4], refs[4:8]
    out_ref, out_vm, sems = refs[8 + held :]
    core, h = scalars[0] & 1, scalars[1]
    gets_fast = (h >> 1) == 1 - core
    tiles = out_vm.shape[0] // ROW_TILE
    width = out_vm.shape[1] // NC

    def copy_of(i):
        rows = pl.ds(pl.multiple_of(i * ROW_TILE, ROW_TILE), ROW_TILE)
        return pltpu.make_async_copy(out_vm.at[rows], out_ref.at[rows], sems.at[i])

    def group(n):
        return pl.ds(n * WIDTH, WIDTH)

    for mine in range(NC):

        @pl.when((core == mine) & (gets_fast == wanted_fast))
        def _(mine=mine):
            def step(i, _):
                rows = pl.ds(pl.multiple_of(i * ROW_TILE, ROW_TILE), ROW_TILE)
                attended = jnp.concatenate([part[rows, :] for part in parts], axis=1)
                for half in range(NC):
                    cols = pl.ds(half * width, width)
                    if half == mine:
                        others = w_one[...], w_two[group(1), :], w_two[group(0), :]
                    else:
                        others = w_swap[group(0), :], w_swap[group(2), :], w_swap[group(1), :]
                    out_vm[rows, cols] = jnp.dot(
                        attended,
                        jnp.concatenate([weight[:, cols], *others], axis=0),
                        preferred_element_type=jnp.float32,
                    ).astype(jnp.bfloat16)
                copy_of(i).start()
                return 0

            lax.fori_loop(0, tiles, step, 0)
            for i in range(tiles):
                copy_of(i).wait()


def project(scalars, parts, weights, wanted_fast, held=None):
    rows, width = CHUNK * BLK, weights[0].shape[1]
    inputs = (*parts, *weights)
    extra = () if held is None else (held,)
    return pl.pallas_call(
        functools.partial(project_kernel, wanted_fast=wanted_fast, held=len(extra)),
        grid_spec=pltpu.PrefetchScalarGridSpec(
            num_scalar_prefetch=1,
            grid=(1,),
            in_specs=[IN_VMEM] * len(inputs) + [IN_HBM] * len(extra),
            out_specs=IN_HBM,
            scratch_shapes=[
                pltpu.VMEM((rows, width), jnp.bfloat16),
                pltpu.SemaphoreType.DMA((rows // ROW_TILE,)),
            ],
        ),
        out_shape=jax.ShapeDtypeStruct((rows, width), jnp.bfloat16),
        input_output_aliases={} if held is None else {1 + len(inputs): 0},
        compiler_params=pltpu.CompilerParams(vmem_limit_bytes=24 * 2**20),
        cost_estimate=pl.CostEstimate(
            flops=2 * rows * NHEAD * WIDTH * width, bytes_accessed=10 * 2**20, transcendentals=0
        ),
    )(scalars, *inputs, *extra)


def per_device(query, keys, values, out_weight, near_list, far_list, stride_table):
    t = lax.axis_index("tm")
    h = lax.axis_index("head")
    coords = [(zz, xx, cc) for zz in range(NZ) for xx in range(NX) for cc in range(NC)]
    swap = [(i, i ^ 1) for i in range(NTM)]
    across = [(i, i + 1) for i in range(1, NTM - 1, 2)]
    across = across + [(j, i) for i, j in across]
    place = jnp.stack([t, h]).astype(jnp.int32)

    thinned, fast_part, slow_part = pack(place, keys, values)
    along_x = [
        lax.ppermute(
            thinned, "tm", [(tm_index(*p), tm_index(p[0], p[1] + d, p[2])) for p in coords]
        )
        for d in range(1, NX)
    ]

    halo_fast = lax.ppermute(fast_part, "tm", swap)
    picks, table = index_work(place, stride_table, far_list, near_list)
    slow_part, table, *along_x = lax.optimization_barrier((slow_part, table, *along_x))
    halo_slow = lax.ppermute(slow_part, "tm", across)

    near_fast = attend(table, query, keys, values, halo_fast, None, FAST_FIRST, 2)
    packs = select(picks, [thinned] + along_x, near_fast[1])
    arrived = [packs[0]]
    for d in range(1, NZ):
        pairs = [(tm_index(*p), tm_index(p[0] + d, p[1], p[2])) for p in coords]
        arrived.append(lax.ppermute(packs[d], "tm", pairs))

    cols = out_weight.shape[1] // NC
    half = lax.dynamic_slice_in_dim(out_weight, (t % NC) * cols, cols, 1)
    half, _ = lax.optimization_barrier((half, table))
    w_one = lax.ppermute(half, "head", [(g, g ^ 1) for g in range(NHEAD)])
    half, w_one, _ = lax.optimization_barrier((half, w_one, packs[0]))
    w_two = lax.ppermute(
        jnp.concatenate([half, w_one], axis=0), "head", [(g, g ^ 3) for g in range(NHEAD)]
    )

    near_slow = attend(
        table, query, keys, values, halo_slow, None, SLOW_FIRST, 2, (packs[0],)
    )
    passed = lax.ppermute(pack_passed(arrived, near_slow[1]), "tm", swap)
    far = [*arrived, passed]
    first_fast, last_fast = merge_far(table, query, near_fast, far, FAST_FIRST, near_slow[1])
    near_slow, first_fast, w_one, w_two = lax.optimization_barrier(
        (near_slow, first_fast, w_one, w_two)
    )
    w_swap = lax.ppermute(jnp.concatenate([w_one, w_two], axis=0), "tm", swap)
    first_slow, last_slow = merge_far(table, query, near_slow, far, SLOW_FIRST, first_fast)

    def exchange(chunk, e, fast):
        pairs = []
        for i in range(NTM):
            frame = (1 - i % NC) if fast else i % NC
            for g in range(NHEAD):
                if (e >= 2) == (g // 2 != frame):
                    pairs.append((i * NHEAD + g, i * NHEAD + (g ^ e)))
        return lax.ppermute(chunk, ("tm", "head"), pairs)

    def received(first, last, fast):
        one, two, three = [
            exchange(chunk, e, fast) for e, chunk in ((1, first), (2, first), (3, last))
        ]
        return last, one, two, three

    weights = (out_weight, w_one, w_two, w_swap)
    fast = received(first_fast, last_fast, True)
    slow = received(first_slow, last_slow, False)
    held = project(place, fast, weights, True)
    return project(place, slow, weights, False, held)


def solution(mesh):
    placed = (
        P("tm", "head"),
        P("tm", "head"),
        P("tm", "head"),
        P("head", None),
        P("tm", None),
        P(),
        P(),
    )
    return jax.shard_map(
        per_device, mesh=mesh, in_specs=placed, out_specs=P(("tm", "head"), None), check_vma=False
    )
```

```python
import functools
import math

import jax
import jax.numpy as jnp
from jax import lax
from jax.experimental import pallas as pl
from jax.experimental.pallas import tpu as pltpu
from jax.sharding import PartitionSpec as P

HD = 128
BLK = 128
FRAME_BLK = 12
KNEAR = 16
KFAR = 16
CAP = 6
MINSTRIDE = 16
THIN = BLK // MINSTRIDE
HEADS = 3
WIDTH = HEADS * HD
BLOCKS = 24
NX, NZ, NC = 4, 4, 2
NTM = NX * NZ * NC
NHEAD = 4
CHUNK = BLOCKS // NHEAD
FAR_ROWS = NTM * CAP * 2 * THIN
FRAME = FRAME_BLK * BLK
LOG2_SCALE = math.log2(math.e) / math.sqrt(HD)
NT = (((1,), (1,)), ((), ()))
VMEM_LIMIT = 56 * 2**20
UNROLL = 6
SLOT, STRIDE, ORDER = KNEAR, KNEAR + KFAR, BLOCKS
FAST_FIRST, FAST_LAST, SLOW_FIRST, SLOW_LAST = range(4)
IN_HBM = pl.BlockSpec(memory_space=pltpu.HBM)
ANYWHERE = pl.BlockSpec(memory_space=pl.ANY)
IN_VMEM = pl.BlockSpec(memory_space=pltpu.VMEM)


def tm_index(z, x, c):
    return (z % NZ) * NX * NC + (x % NX) * NC + c


def load_far(far_refs, far_vm, sems, first_sem):
    part = NX * CAP * 2 * THIN
    copies = []
    for n, ref in enumerate(far_refs):
        rows = part if n < NZ else NZ * part
        copies.append(
            pltpu.make_async_copy(
                ref.at[pl.ds(0, rows)], far_vm.at[pl.ds(n * part, rows)], sems.at[first_sem + n]
            )
        )
    return copies


def far_block(far_vm, table, block):
    tiles = [
        far_vm[
            pl.ds(pl.multiple_of(table[block, SLOT + j] * 2 * THIN, 2 * THIN), 2 * THIN), :
        ].astype(jnp.float32)
        for j in range(KFAR)
    ]
    keys = jnp.concatenate([t[:THIN] for t in tiles], axis=0).astype(jnp.bfloat16)
    values = jnp.concatenate([t[THIN:] for t in tiles], axis=0).astype(jnp.bfloat16)
    lane = lax.broadcasted_iota(jnp.int32, (1, BLK), 1)
    stride = jnp.zeros((1, BLK), jnp.int32)
    for j in range(KFAR):
        stride = jnp.where(lane // THIN == j, table[block, STRIDE + j], stride)
    used = (((lane % THIN) * MINSTRIDE) & (stride - 1)) == 0
    return keys, values, used


def with_ones(values):
    return jnp.concatenate([values, jnp.ones((values.shape[0], HD), jnp.bfloat16)], axis=1)


def attend_kernel(table, q_ref, k_ref, v_ref, halo_ref, *rest, chunk, with_far, ordering):
    rest = rest[ordering:]
    if with_far:
        far_refs, (out_ref, k_vm, v_vm, s_vm, far_vm, sems) = rest[:5], rest[5:]
    else:
        near_ref, level_ref, k_vm, v_vm, s_vm, sems = rest
    step = pl.program_id(0)
    own = BLOCKS * BLK
    halo = pl.ds(own, FRAME)
    key_copies = [
        pltpu.make_async_copy(k_ref, k_vm.at[pl.ds(0, own)], sems.at[0]),
        pltpu.make_async_copy(halo_ref.at[pl.ds(0, FRAME)], k_vm.at[halo], sems.at[1]),
    ]
    value_copies = [
        pltpu.make_async_copy(v_ref, v_vm.at[pl.ds(0, own)], sems.at[2]),
        pltpu.make_async_copy(halo_ref.at[pl.ds(FRAME, FRAME)], v_vm.at[halo], sems.at[3]),
    ]
    if with_far:
        key_copies += load_far(far_refs, far_vm, sems, 4)

    @pl.when(step == 0)
    def _():
        for copy in key_copies + value_copies:
            copy.start()
        for copy in key_copies:
            copy.wait()

    first = table[ORDER, chunk + step] * CHUNK

    def prepare(unit):
        block = first + unit
        offsets = [pl.multiple_of(table[block, j] * BLK, BLK) for j in range(KNEAR)]
        far = far_block(far_vm, table, block) if with_far else None
        return offsets, far, pl.ds(pl.multiple_of(unit * BLK, BLK), BLK)

    count = KNEAR + (1 if with_far else 0)

    def score_pair(prepared, head, j):
        offsets, far, rows = prepared
        cols = slice(head * HD, head * HD + HD)
        query = q_ref[rows, cols]
        if j < KNEAR:
            keys = jnp.concatenate([k_vm[pl.ds(o, BLK), cols] for o in offsets[j : j + 2]], axis=0)
            both = lax.dot_general(query, keys, NT, preferred_element_type=jnp.float32)
            return [both[:, :BLK], both[:, BLK:]]
        last = lax.dot_general(query, far[0][:, cols], NT, preferred_element_type=jnp.float32)
        return [jnp.where(far[2], last, -1e30)]

    def peak_of(scores):
        top = functools.reduce(jnp.maximum, scores)
        return jnp.max(top, axis=1, keepdims=True) * LOG2_SCALE

    def add_pair(acc, prepared, head, scores, peak, j):
        offsets, far, _ = prepared
        cols = slice(head * HD, head * HD + HD)
        some = range(j, min(j + 2, count))
        weights = jnp.concatenate(
            [jnp.exp2(scores[i] * LOG2_SCALE - peak).astype(jnp.bfloat16) for i in some], axis=1
        )
        values = jnp.concatenate(
            [v_vm[pl.ds(offsets[i], BLK), cols] if i < KNEAR else far[1][:, cols] for i in some],
            axis=0,
        )
        part = jnp.dot(weights, with_ones(values), preferred_element_type=jnp.float32)
        return part if acc is None else acc + part

    def store(prepared, head, peak, acc):
        rows = prepared[2]
        cols = slice(head * HD, head * HD + HD)
        if with_far:
            out_ref[rows, cols] = (acc[:, :HD] / acc[:, HD:]).astype(jnp.bfloat16)
        else:
            near_ref[rows, cols] = (acc[:, :HD] / acc[:, HD:]).astype(jnp.bfloat16)
            level_ref[rows, cols] = peak + jnp.log2(acc[:, HD:])

    def scores_of(prepared, head):
        scores = []
        for j in range(0, count, 2):
            scores += score_pair(prepared, head, j)
        return scores

    def overlap(fresh, pending):
        prepared, head, scores = pending
        peak = peak_of(scores)
        following, acc = [], None
        for j in range(0, count, 2):
            following += score_pair(*fresh, j)
            acc = add_pair(acc, prepared, head, scores, peak, j)
        store(prepared, head, peak, acc)
        return following

    def hold(scores):
        for i, some in enumerate(scores):
            s_vm[:, i * BLK : i * BLK + BLK] = some

    hold(scores_of(prepare(0), 0))

    @pl.when(step == 0)
    def _():
        for copy in value_copies:
            copy.wait()

    units = CHUNK // UNROLL

    def body(i, _):
        pending = None
        scores = [s_vm[:, n * BLK : n * BLK + BLK] for n in range(count)]
        for u in range(UNROLL):
            unit = i * UNROLL + u
            prepared = prepare(unit)
            for head in range(HEADS):
                if head or u:
                    scores = overlap((prepared, head), pending)
                pending = prepared, head, scores
        after = prepare(jnp.minimum(i * UNROLL + UNROLL, CHUNK - 1))
        hold(overlap((after, 0), pending))
        return 0

    lax.fori_loop(0, units, body, 0)


def attend(table, query, keys, values, halo, far, chunk, chunks, after=()):
    with_far = far is not None
    spot = lambda i, s: (s[ORDER, chunk + i], 0)
    same = lambda i, s: (i, 0)
    rows = CHUNK * BLK
    scratch = [pltpu.VMEM((BLOCKS * BLK + FRAME, WIDTH), jnp.bfloat16) for _ in range(2)]
    scratch.append(pltpu.VMEM((BLK, (KNEAR + 1) * BLK), jnp.float32))
    if with_far:
        scratch.append(pltpu.VMEM((FAR_ROWS, WIDTH), jnp.bfloat16))
        out_shape = jax.ShapeDtypeStruct((chunks * rows, WIDTH), jnp.bfloat16)
        out_specs = pl.BlockSpec((rows, WIDTH), same)
    else:
        out_shape = [
            jax.ShapeDtypeStruct((chunks * rows, WIDTH), kind)
            for kind in (jnp.bfloat16, jnp.float32)
        ]
        out_specs = [pl.BlockSpec((rows, WIDTH), same)] * 2
    scratch.append(pltpu.SemaphoreType.DMA((9,)))
    extra = tuple(far) if with_far else ()
    return pl.pallas_call(
        functools.partial(
            attend_kernel, chunk=chunk, with_far=with_far, ordering=len(after)
        ),
        grid_spec=pltpu.PrefetchScalarGridSpec(
            num_scalar_prefetch=1,
            grid=(chunks,),
            in_specs=[pl.BlockSpec((rows, WIDTH), spot)] + [IN_HBM] * 3 + [ANYWHERE] * len(after + extra),
            out_specs=out_specs,
            scratch_shapes=scratch,
        ),
        out_shape=out_shape,
        compiler_params=pltpu.CompilerParams(vmem_limit_bytes=VMEM_LIMIT),
        cost_estimate=pl.CostEstimate(
            flops=chunks * CHUNK * HEADS * 17 * 4 * BLK * BLK * HD * 3,
            bytes_accessed=8 * 2**20,
            transcendentals=0,
        ),
    )(table, query, keys, values, halo, *after, *extra)


def merge_kernel(table, q_ref, near_ref, level_ref, *rest, chunk):
    far_refs, (_, first_ref, last_ref, out_vm, far_vm, sems) = rest[:5], rest[5:]
    step = pl.program_id(0)

    @pl.when(step == 0)
    def _():
        copies = load_far(far_refs, far_vm, sems, 0)
        for copy in copies:
            copy.start()
        for copy in copies:
            copy.wait()

    first = table[ORDER, chunk + step] * CHUNK
    spot = {
        (unit, head): (
            slice(unit * BLK, unit * BLK + BLK),
            slice(head * HD, head * HD + HD),
        )
        for unit in range(CHUNK)
        for head in range(HEADS)
    }
    far = [far_block(far_vm, table, first + unit) for unit in range(CHUNK)]
    scores, peaks, sums = {}, {}, {}
    for p, (rows, cols) in spot.items():
        keys, _, used = far[p[0]]
        some = lax.dot_general(
            q_ref[rows, cols], keys[:, cols], NT, preferred_element_type=jnp.float32
        )
        scores[p] = jnp.where(used, some, -1e30) * LOG2_SCALE
    for p, (rows, cols) in spot.items():
        peaks[p] = jnp.maximum(jnp.max(scores[p], axis=1, keepdims=True), level_ref[rows, cols])
    for p, (rows, cols) in spot.items():
        weights = jnp.exp2(scores[p] - peaks[p]).astype(jnp.bfloat16)
        values = far[p[0]][1][:, cols]
        sums[p] = jnp.dot(weights, with_ones(values), preferred_element_type=jnp.float32)
    for p, (rows, cols) in spot.items():
        share = jnp.exp2(level_ref[rows, cols] - peaks[p])
        total = share + sums[p][:, HD:]
        mixed = near_ref[rows, cols].astype(jnp.float32) * share + sums[p][:, :HD]
        out_vm[step, rows, cols] = (mixed / total).astype(jnp.bfloat16)

    outs = [
        pltpu.make_async_copy(out_vm.at[n], ref, sems.at[5 + n])
        for n, ref in enumerate((first_ref, last_ref))
    ]

    @pl.when(step == 0)
    def _():
        outs[0].start()

    @pl.when(step == 1)
    def _():
        outs[1].start()
        for copy in outs:
            copy.wait()


def merge_far(table, query, state, far, chunk, after):
    rows = CHUNK * BLK
    return pl.pallas_call(
        functools.partial(merge_kernel, chunk=chunk),
        grid_spec=pltpu.PrefetchScalarGridSpec(
            num_scalar_prefetch=1,
            grid=(2,),
            in_specs=[pl.BlockSpec((rows, WIDTH), lambda i, s: (s[ORDER, chunk + i], 0))]
            + [pl.BlockSpec((rows, WIDTH), lambda i, s: (i, 0))] * 2
            + [ANYWHERE] * 6,
            out_specs=[IN_HBM] * 2,
            scratch_shapes=[
                pltpu.VMEM((2, rows, WIDTH), jnp.bfloat16),
                pltpu.VMEM((FAR_ROWS, WIDTH), jnp.bfloat16),
                pltpu.SemaphoreType.DMA((7,)),
            ],
        ),
        out_shape=[jax.ShapeDtypeStruct((rows, WIDTH), jnp.bfloat16)] * 2,
        compiler_params=pltpu.CompilerParams(vmem_limit_bytes=VMEM_LIMIT),
        cost_estimate=pl.CostEstimate(
            flops=2 * CHUNK * HEADS * 4 * BLK * BLK * HD * 6,
            bytes_accessed=8 * 2**20,
            transcendentals=0,
        ),
    )(table, query, *state, *far, after)


def index_kernel(scalars, steps, far_ref, near_ref, picks_ref, table_ref):
    t = scalars[0]
    core, x, z = t & 1, (t >> 1) & 3, t >> 3
    lane = lax.broadcasted_iota(jnp.int32, (1, BLK), 1)
    group = (lane * 2731) >> 16
    within = lane - group * BLOCKS
    valid = lane < NX * BLOCKS

    source = ((z * NX + ((x - group) & 3)) * NC + core) * BLOCKS + within
    source = jnp.where(valid, source, -1)
    present = []
    for dz in range(NZ):
        for dc in range(NC):
            receiver = (((z + dz) & 3) * NX + x) * NC + (core ^ dc)
            listed = far_ref[pl.ds(pl.multiple_of(receiver * BLOCKS, 8), BLOCKS), :]
            found = jnp.zeros((BLOCKS, BLK), jnp.float32)
            for j in range(KFAR):
                found = jnp.where(listed[:, j : j + 1] == source, 1.0, found)
            present.append(jnp.max(found, axis=0, keepdims=True))

    mine = far_ref[pl.ds(pl.multiple_of(t * BLOCKS, 8), BLOCKS), :]
    ids = [jnp.where(valid, row * NX * BLOCKS + lane, -1) for row in range(NTM // NX)]
    found = [jnp.zeros((BLOCKS, BLK), jnp.float32) for _ in ids]
    for j in range(KFAR):
        column = jnp.broadcast_to(mine[:, j : j + 1], (BLOCKS, BLK))
        found = [jnp.where(column == i, 1.0, f) for i, f in zip(ids, found)]
    present += [jnp.max(f, axis=0, keepdims=True) for f in found]
    present = jnp.concatenate(present, axis=0)

    a = lax.broadcasted_iota(jnp.int32, (BLK, BLK), 0)
    b = lax.broadcasted_iota(jnp.int32, (BLK, BLK), 1)
    group_a, group_b = (a * 2731) >> 16, (b * 2731) >> 16
    before = jnp.where((group_a == group_b) & (a < b), 1.0, 0.0).astype(jnp.bfloat16)
    rank = jnp.dot(present.astype(jnp.bfloat16), before, preferred_element_type=jnp.float32)

    receivers = NZ * NC
    chosen = [
        jnp.where((present[:receivers] > 0) & (rank[:receivers] == k), within.astype(jnp.float32), 0.0)
        for k in range(CAP)
    ]
    gather = jnp.where(group_a == b, 1.0, 0.0).astype(jnp.bfloat16)
    picks = jnp.dot(
        jnp.concatenate(chosen, axis=0).astype(jnp.bfloat16),
        gather,
        preferred_element_type=jnp.float32,
    )
    picks_ref[...] = picks.astype(jnp.int32)

    lies = []
    for row in range(NTM // NX):
        device = row * NX + group
        dz = (z - (device >> 3)) & 3
        dx = (x - (device >> 1)) & 3
        dc = core ^ (device & 1)
        start = ((dc * NZ + dz) * NX + dx) * CAP
        lies.append(start.astype(jnp.float32) + rank[receivers + row : receivers + row + 1])
    entry = lax.broadcasted_iota(jnp.int32, (BLOCKS, KFAR), 1)
    slots = jnp.zeros((BLOCKS, KFAR), jnp.float32)
    for j in range(KFAR):
        column = jnp.broadcast_to(mine[:, j : j + 1], (BLOCKS, BLK))
        at = jnp.zeros((BLOCKS, BLK), jnp.float32)
        for i, where in zip(ids, lies):
            at = jnp.where(column == i, where, at)
        slots = jnp.where(entry == j, jnp.sum(at, axis=1, keepdims=True), slots)

    row = lax.broadcasted_iota(jnp.int32, (BLOCKS, KFAR), 0)
    frame = t * (BLOCKS // FRAME_BLK) + jnp.where(row >= FRAME_BLK, 1, 0)
    distance = jnp.abs(frame - ((mine * 5462) >> 16))
    strides = jnp.zeros((BLOCKS, KFAR), jnp.int32)
    for d in range(steps.shape[0]):
        strides = jnp.where(distance == d, steps[d], strides)

    local = near_ref[...] - t * BLOCKS
    local = jnp.where(local < 0, local + FRAME_BLK + BLOCKS, local)
    rest = jnp.zeros((BLOCKS, BLK - KNEAR - 2 * KFAR), jnp.int32)
    table_ref[:BLOCKS, :] = jnp.concatenate(
        [local, slots.astype(jnp.int32), strides, rest], axis=1
    )

    h = scalars[1]
    order = jnp.zeros((8, BLK), jnp.int32)
    column = lax.broadcasted_iota(jnp.int32, (8, BLK), 1)
    for at, half in ((FAST_FIRST, 1 - core), (SLOW_FIRST, core)):
        inside = (h >> 1) == half
        order = jnp.where(column == at, jnp.where(inside, h ^ 1, h ^ 2), order)
        order = jnp.where(column == at + 1, jnp.where(inside, h, h ^ 3), order)
    table_ref[BLOCKS:, :] = order


def index_work(scalars, steps, far_list, near_list):
    whole = lambda shape: pl.BlockSpec(shape, lambda i, *_: (0, 0))
    shapes = [(NZ * NC * CAP, BLK), (BLOCKS + 8, BLK)]
    return pl.pallas_call(
        index_kernel,
        grid_spec=pltpu.PrefetchScalarGridSpec(
            num_scalar_prefetch=2,
            grid=(1,),
            in_specs=[whole(far_list.shape), whole(near_list.shape)],
            out_specs=[whole(shape) for shape in shapes],
        ),
        out_shape=[jax.ShapeDtypeStruct(shape, jnp.int32) for shape in shapes],
        cost_estimate=pl.CostEstimate(flops=2**20, bytes_accessed=2**22, transcendentals=0),
    )(scalars, steps, far_list, near_list)


def pack_kernel(scalars, k_fast, v_fast, k_slow, v_slow, thin_ref, fast_ref, slow_ref):
    core, step = scalars[0] & 1, pl.program_id(0)
    blocks = k_fast.shape[0] // BLK

    def thin(ref):
        rows = ref[...].astype(jnp.float32).reshape(blocks * THIN, MINSTRIDE, WIDTH)
        return rows[:, 0, :]

    for out, frame, k_part, v_part in (
        (fast_ref, 1 - core, k_fast, v_fast),
        (slow_ref, core, k_slow, v_slow),
    ):
        out[0] = k_part[...]
        out[1] = v_part[...]
        keys, values = thin(k_part), thin(v_part)
        pairs = [a[b * THIN : b * THIN + THIN] for b in range(blocks) for a in (keys, values)]
        first = (frame * FRAME_BLK + step * blocks) * 2 * THIN
        rows = pl.ds(pl.multiple_of(first, 2 * THIN), blocks * 2 * THIN)
        thin_ref[rows, :] = jnp.concatenate(pairs, axis=0).astype(jnp.bfloat16)


def pack(scalars, keys, values):
    parts = 4
    rows = FRAME // parts
    fast = pl.BlockSpec((rows, WIDTH), lambda i, s: ((1 - (s[0] & 1)) * parts + i, 0))
    slow = pl.BlockSpec((rows, WIDTH), lambda i, s: ((s[0] & 1) * parts + i, 0))
    frame = jax.ShapeDtypeStruct((2, FRAME, WIDTH), jnp.bfloat16)
    thinned = jax.ShapeDtypeStruct((BLOCKS * 2 * THIN, WIDTH), jnp.bfloat16)
    thinned, *frames = pl.pallas_call(
        pack_kernel,
        grid_spec=pltpu.PrefetchScalarGridSpec(
            num_scalar_prefetch=1,
            grid=(parts,),
            in_specs=[fast, fast, slow, slow],
            out_specs=[pl.BlockSpec(thinned.shape, lambda i, s: (0, 0))]
            + [pl.BlockSpec((2, rows, WIDTH), lambda i, s: (0, i, 0))] * 2,
        ),
        out_shape=[thinned, frame, frame],
        cost_estimate=pl.CostEstimate(flops=0, bytes_accessed=10 * 2**20, transcendentals=0),
    )(scalars, keys, values, keys, values)
    return thinned, *(f.reshape(2 * FRAME, WIDTH) for f in frames)


def pass_kernel(a, b, c, d, after, out_ref):
    rows = a.shape[0]
    for n, ref in enumerate((a, b, c, d)):
        out_ref[n * rows : n * rows + rows, :] = ref[...]


def pack_passed(arrived, after):
    rows = arrived[0].shape[0] // 2
    return pl.pallas_call(
        pass_kernel,
        grid=(1,),
        in_specs=[pl.BlockSpec((rows, WIDTH), lambda i: (1, 0))] * NZ + [ANYWHERE],
        out_specs=pl.BlockSpec((NZ * rows, WIDTH), lambda i: (0, 0)),
        out_shape=jax.ShapeDtypeStruct((NZ * rows, WIDTH), jnp.bfloat16),
        cost_estimate=pl.CostEstimate(flops=0, bytes_accessed=2 * 2**20, transcendentals=0),
    )(*arrived, after)


def select_kernel(picks, *refs):
    sources, outs = refs[:NX], refs[NX + 1 :]
    for dz, out in enumerate(outs):
        for dc in range(NC):
            for s in range(NX):
                for k in range(CAP):
                    block = picks[k * NZ * NC + dz * NC + dc, s]
                    at = pl.ds(pl.multiple_of(block * 2 * THIN, 2 * THIN), 2 * THIN)
                    to = ((dc * NX + s) * CAP + k) * 2 * THIN
                    out[to : to + 2 * THIN, :] = sources[s][at, :]


def select(picks, sources, after):
    shape = jax.ShapeDtypeStruct((NC * NX * CAP * 2 * THIN, WIDTH), jnp.bfloat16)
    whole = lambda a: pl.BlockSpec(a.shape, lambda i, *_: (0, 0))
    return pl.pallas_call(
        select_kernel,
        grid_spec=pltpu.PrefetchScalarGridSpec(
            num_scalar_prefetch=1,
            grid=(1,),
            in_specs=[whole(s) for s in sources] + [ANYWHERE],
            out_specs=[whole(shape)] * NZ,
        ),
        out_shape=[shape] * NZ,
        compiler_params=pltpu.CompilerParams(vmem_limit_bytes=VMEM_LIMIT),
        cost_estimate=pl.CostEstimate(flops=0, bytes_accessed=4 * 2**20, transcendentals=0),
    )(picks, *sources, after)


ROW_TILE = 256


def project_kernel(scalars, *refs, wanted_fast, held):
    parts, (weight, w_one, w_two, w_swap) = refs[:4], refs[4:8]
    out_ref, out_vm, sems = refs[8 + held :]
    core, h = scalars[0] & 1, scalars[1]
    gets_fast = (h >> 1) == 1 - core
    tiles = out_vm.shape[0] // ROW_TILE
    width = out_vm.shape[1] // NC

    def copy_of(i):
        rows = pl.ds(pl.multiple_of(i * ROW_TILE, ROW_TILE), ROW_TILE)
        return pltpu.make_async_copy(out_vm.at[rows], out_ref.at[rows], sems.at[i])

    def group(n):
        return pl.ds(n * WIDTH, WIDTH)

    for mine in range(NC):

        @pl.when((core == mine) & (gets_fast == wanted_fast))
        def _(mine=mine):
            def step(i, _):
                rows = pl.ds(pl.multiple_of(i * ROW_TILE, ROW_TILE), ROW_TILE)
                attended = jnp.concatenate([part[rows, :] for part in parts], axis=1)
                for half in range(NC):
                    cols = pl.ds(half * width, width)
                    if half == mine:
                        others = w_one[...], w_two[group(1), :], w_two[group(0), :]
                    else:
                        others = w_swap[group(0), :], w_swap[group(2), :], w_swap[group(1), :]
                    out_vm[rows, cols] = jnp.dot(
                        attended,
                        jnp.concatenate([weight[:, cols], *others], axis=0),
                        preferred_element_type=jnp.float32,
                    ).astype(jnp.bfloat16)
                copy_of(i).start()
                return 0

            lax.fori_loop(0, tiles, step, 0)
            for i in range(tiles):
                copy_of(i).wait()


def project(scalars, parts, weights, wanted_fast, held=None):
    rows, width = CHUNK * BLK, weights[0].shape[1]
    inputs = (*parts, *weights)
    extra = () if held is None else (held,)
    return pl.pallas_call(
        functools.partial(project_kernel, wanted_fast=wanted_fast, held=len(extra)),
        grid_spec=pltpu.PrefetchScalarGridSpec(
            num_scalar_prefetch=1,
            grid=(1,),
            in_specs=[IN_VMEM] * len(inputs) + [IN_HBM] * len(extra),
            out_specs=IN_HBM,
            scratch_shapes=[
                pltpu.VMEM((rows, width), jnp.bfloat16),
                pltpu.SemaphoreType.DMA((rows // ROW_TILE,)),
            ],
        ),
        out_shape=jax.ShapeDtypeStruct((rows, width), jnp.bfloat16),
        input_output_aliases={} if held is None else {1 + len(inputs): 0},
        compiler_params=pltpu.CompilerParams(vmem_limit_bytes=24 * 2**20),
        cost_estimate=pl.CostEstimate(
            flops=2 * rows * NHEAD * WIDTH * width, bytes_accessed=10 * 2**20, transcendentals=0
        ),
    )(scalars, *inputs, *extra)


def per_device(query, keys, values, out_weight, near_list, far_list, stride_table):
    t = lax.axis_index("tm")
    h = lax.axis_index("head")
    coords = [(zz, xx, cc) for zz in range(NZ) for xx in range(NX) for cc in range(NC)]
    swap = [(i, i ^ 1) for i in range(NTM)]
    across = [(i, i + 1) for i in range(1, NTM - 1, 2)]
    across = across + [(j, i) for i, j in across]
    place = jnp.stack([t, h]).astype(jnp.int32)

    thinned, fast_part, slow_part = pack(place, keys, values)
    along_x = [
        lax.ppermute(
            thinned, "tm", [(tm_index(*p), tm_index(p[0], p[1] + d, p[2])) for p in coords]
        )
        for d in range(1, NX)
    ]

    halo_fast = lax.ppermute(fast_part, "tm", swap)
    picks, table = index_work(place, stride_table, far_list, near_list)
    slow_part, table, *along_x = lax.optimization_barrier((slow_part, table, *along_x))
    halo_slow = lax.ppermute(slow_part, "tm", across)

    near_fast = attend(table, query, keys, values, halo_fast, None, FAST_FIRST, 2)
    packs = select(picks, [thinned] + along_x, near_fast[1])
    arrived = [packs[0]]
    for d in range(1, NZ):
        pairs = [(tm_index(*p), tm_index(p[0] + d, p[1], p[2])) for p in coords]
        arrived.append(lax.ppermute(packs[d], "tm", pairs))

    cols = out_weight.shape[1] // NC
    half = lax.dynamic_slice_in_dim(out_weight, (t % NC) * cols, cols, 1)
    half, _ = lax.optimization_barrier((half, table))
    w_one = lax.ppermute(half, "head", [(g, g ^ 1) for g in range(NHEAD)])
    half, w_one, _ = lax.optimization_barrier((half, w_one, packs[0]))
    w_two = lax.ppermute(
        jnp.concatenate([half, w_one], axis=0), "head", [(g, g ^ 3) for g in range(NHEAD)]
    )

    near_slow = attend(
        table, query, keys, values, halo_slow, None, SLOW_FIRST, 2, (packs[0],)
    )
    passed = lax.ppermute(pack_passed(arrived, near_slow[1]), "tm", swap)
    far = [*arrived, passed]
    w_swap = lax.ppermute(jnp.concatenate([w_one, w_two], axis=0), "tm", swap)
    first_fast, last_fast = merge_far(table, query, near_fast, far, FAST_FIRST, near_slow[1])
    near_slow, first_fast = lax.optimization_barrier((near_slow, first_fast))
    first_slow, last_slow = merge_far(table, query, near_slow, far, SLOW_FIRST, w_swap)

    def exchange(chunk, e, fast):
        pairs = []
        for i in range(NTM):
            frame = (1 - i % NC) if fast else i % NC
            for g in range(NHEAD):
                if (e >= 2) == (g // 2 != frame):
                    pairs.append((i * NHEAD + g, i * NHEAD + (g ^ e)))
        return lax.ppermute(chunk, ("tm", "head"), pairs)

    def received(first, last, fast):
        one, two, three = [
            exchange(chunk, e, fast) for e, chunk in ((1, first), (2, first), (3, last))
        ]
        return last, one, two, three

    weights = (out_weight, w_one, w_two, w_swap)
    fast = received(first_fast, last_fast, True)
    slow = received(first_slow, last_slow, False)
    held = project(place, fast, weights, True)
    return project(place, slow, weights, False, held)


def solution(mesh):
    placed = (
        P("tm", "head"),
        P("tm", "head"),
        P("tm", "head"),
        P("head", None),
        P("tm", None),
        P(),
        P(),
    )
    return jax.shard_map(
        per_device, mesh=mesh, in_specs=placed, out_specs=P(("tm", "head"), None), check_vma=False
    )
```
